32 devices in a mesh: docs: 16 (over z, x, core), half: 2 (over y).
Axes of the slice: x: 2, y: 2, z: 4, core: 2. Of those that a mesh axis runs over, the one named last changes fastest.
Arguments:
- hidden_in: bfloat16 [32, 1024, 768], P('docs', 'half'), may hold values from -6 to 6
- boxes: int32 [4, 32, 1024], P(None, 'docs'), may hold values from 0 to 999
- lengths: int32 [32], P('docs'), may hold values from 640 to 1024, as said below
- cotangent: bfloat16 [32, 1024, 768], P('docs', 'half'), may hold values from -6 to 6
- layout_weight: bfloat16 [128, 768], replicated, may hold values from -0.5 to 0.5
- qkv_weight: bfloat16 [768, 2304], replicated, may hold values from -0.21875 to 0.21875
- qv_bias: bfloat16 [2, 768], replicated, may hold values from -3 to 3
- bias_tables: bfloat16 [3, 32, 12], replicated, may hold values from -4 to 4
- out_weight: bfloat16 [768, 768], replicated, may hold values from -0.625 to 0.625
- out_bias: bfloat16 [768], replicated, may hold values from -3 to 3
- norm1_gain: bfloat16 [768], replicated, may hold values from 0.5 to 1.5
- norm1_bias: bfloat16 [768], replicated, may hold values from -3 to 3
- ff_in: bfloat16 [768, 3072], replicated, may hold values from -0.21875 to 0.21875
- ff_in_bias: bfloat16 [3072], replicated, may hold values from -3 to 3
- ff_out: bfloat16 [3072, 768], replicated, may hold values from -0.109375 to 0.109375
- ff_out_bias: bfloat16 [768], replicated, may hold values from -3 to 3
- norm2_gain: bfloat16 [768], replicated, may hold values from 0.5 to 1.5
- norm2_bias: bfloat16 [768], replicated, may hold values from -3 to 3
Outputs:
- layer_out: bfloat16 [32, 1024, 768], P('docs', 'half')
- input_grad: bfloat16 [32, 1024, 768], P('docs', 'half')
- layout_weight_grad: float32 [128, 768], replicated
- qkv_weight_grad: float32 [768, 2304], replicated
- qv_bias_grad: float32 [2, 768], replicated
- bias_tables_grad: float32 [3, 32, 12], replicated
- out_weight_grad: float32 [768, 768], replicated
- out_bias_grad: float32 [768], replicated
- norm1_gain_grad: float32 [768], replicated
- norm1_bias_grad: float32 [768], replicated
- ff_in_grad: float32 [768, 3072], replicated
- ff_in_bias_grad: float32 [3072], replicated
- ff_out_grad: float32 [3072, 768], replicated
- ff_out_bias_grad: float32 [768], replicated
- norm2_gain_grad: float32 [768], replicated
- norm2_bias_grad: float32 [768], replicated
The draws below stay inside these ranges and needn't reach their ends.
Inputs may be any that keep to these rules, and one draw needn't show every extreme that they name: `lengths`: one sequence, which one drawn from the seed, has length 1024.
All inputs are finite; a program needn't handle non-finite values.
Results may differ from the reference program's by a relative error of at most 0.015.
Values may be sent and summed in bfloat16 or wider, within the bound.
No kernel may reach another device: no remote copies, remote signals or barrier semaphores. Data moves between devices by JAX's collectives and lax.ppermute only.
A program may use at most 384 MiB of HBM per device.

```python
import math
import jax
import jax.numpy as jnp
from jax import lax

D = 768
HEADS = 12
HEAD_DIM = 64
FF = 3072
BUCKETS = 32
FEATS = 128
BOXQ = 1000
LEN = 1024
HALF = 512
NSEQ = 32


def draw_lengths(key, part):
    key = jax.random.fold_in(key, 11)
    first_key, second_key = jax.random.split(key)
    base = jax.random.randint(first_key, (NSEQ,), HALF + LEN // 8, LEN + 1)
    pick = jax.random.randint(second_key, (), 0, NSEQ)
    chosen = jnp.arange(NSEQ, dtype=jnp.int32) == pick
    return jnp.where(chosen, LEN, base).astype(jnp.int32)


def touch_ends(array, rng, low, top_value):
    longest = array.shape.index(max(array.shape))
    spots = []
    for shift in (0, 1):
        where = [jax.random.randint(jax.random.fold_in(rng, axis), (), 0, length) for axis, length in enumerate(array.shape)]
        where[longest] = (where[longest] + shift) % array.shape[longest]
        spots.append(tuple(where))
    return array.at[spots[0]].set(low).at[spots[1]].set(top_value)


def steps_of(key, extent, pieces, low, high):
    def one(position, shards_of):
        steps = jax.random.uniform(jax.random.fold_in(jax.random.fold_in(key, 6), position), (shards_of,), jnp.float32, low / len(pieces), high / len(pieces))
        return jnp.repeat(jnp.exp(steps), extent[position] // shards_of).reshape((-1,) + (1,) * (len(extent) - position - 1))

    factor_of = one(*pieces[0])
    for cut in pieces[1:]:
        factor_of = factor_of * one(*cut)
    return factor_of


def centred(rng, extent, width, reach, cuts=(), kind=jnp.bfloat16):
    array = jax.random.normal(rng, extent, jnp.float32) * width
    if len(cuts) > 0:
        array = steps_of(rng, extent, cuts, -0.22, 0.18) * array
    return jnp.clip(array, min=-reach, max=reach).astype(kind)


def setup_inputs(seed: int = 0) -> dict:
    seeds = jax.random.split(jax.random.key(seed), 19)
    return {
        "hidden_in": centred(seeds[0], (NSEQ, LEN, D), 1.0, 6.0, ((0, 16), (1, 2))),
        "boxes": touch_ends(jax.random.randint(seeds[1], (4, NSEQ, LEN), 0, BOXQ), jax.random.fold_in(seeds[1], 1), 0, BOXQ - 1).astype(jnp.int32),
        "lengths": draw_lengths(jax.random.fold_in(seeds[18], 71), 0),
        "cotangent": centred(seeds[3], (NSEQ, LEN, D), 1.0, 6.0, ((0, 16), (1, 2))),
        "layout_weight": centred(seeds[4], (FEATS, D), FEATS ** -0.5, 0.5),
        "qkv_weight": centred(seeds[5], (D, 3 * D), D ** -0.5, 0.21875),
        "qv_bias": centred(seeds[6], (2, D), 0.5, 3.0),
        "bias_tables": centred(seeds[7], (3, BUCKETS, HEADS), 1.0, 4.0),
        "out_weight": centred(seeds[8], (D, D), (D // 8) ** -0.5, 0.625),
        "out_bias": centred(seeds[9], (D,), 0.5, 3.0),
        "norm1_gain": jnp.clip(1.0 + 0.1 * jax.random.normal(seeds[10], (D,), jnp.float32), 0.5, 1.5).astype(jnp.bfloat16),
        "norm1_bias": centred(seeds[11], (D,), 0.5, 3.0),
        "ff_in": centred(seeds[12], (D, FF), D ** -0.5, 0.21875),
        "ff_in_bias": centred(seeds[13], (FF,), 0.5, 3.0),
        "ff_out": centred(seeds[14], (FF, D), FF ** -0.5, 0.109375),
        "ff_out_bias": centred(seeds[15], (D,), 0.5, 3.0),
        "norm2_gain": jnp.clip(1.0 + 0.1 * jax.random.normal(seeds[16], (D,), jnp.float32), 0.5, 1.5).astype(jnp.bfloat16),
        "norm2_bias": centred(seeds[17], (D,), 0.5, 3.0),
    }


NEAR_EDGES = (1, 2, 3, 4, 5, 6, 7, 8, 12, 16, 24, 32, 64, 128, 256)
FAR_EDGES = (1, 2, 4, 8, 16, 32, 64, 96, 128, 192, 256, 384, 512, 768, 1024)

@jax.custom_vjp
def low(v):
    return lax.optimization_barrier(v.astype(jnp.bfloat16)).astype(jnp.float32)

@jax.custom_vjp
def low_back(v):
    return v

def low_keep(v):
    return (low(v), None)

def low_pass(kept, grad):
    return (grad,)

def back_keep(v):
    return (v, None)

def back_low(kept, grad):
    return (low(grad),)
low.defvjp(low_keep, low_pass)
low_back.defvjp(back_keep, back_low)

def matmul(left, right):
    return jnp.dot(left, right, precision=lax.Precision.HIGHEST)

def fourier(coords):
    scaled = coords.astype(jnp.float32) / BOXQ
    freqs = (jnp.arange(16, dtype=jnp.float32) + 1.0) * math.pi
    angle = scaled[:, :, None] * freqs[None, None, :]
    waves = jnp.concatenate([jnp.sin(angle), jnp.cos(angle)], axis=2)
    return jnp.transpose(waves, (1, 0, 2)).reshape(coords.shape[1], 128)

def level(rel, edges):
    magnitude = jnp.abs(rel)
    result = jnp.zeros(rel.shape, jnp.int32)
    for edge in edges:
        result = result + (magnitude >= edge).astype(jnp.int32)
    return result + 16 * (rel > 0).astype(jnp.int32)

def layer_norm(resid, gain, shift):
    centre = resid - lax.optimization_barrier(jnp.mean(resid, axis=-1, keepdims=True))
    spread = lax.optimization_barrier(jnp.mean(centre * centre, axis=-1, keepdims=True))
    return centre * lax.rsqrt(spread + 1e-06) * gain + shift

def layer(params, hidden, box, length):
    lay_w, qkv_w, qv_b, tables, out_w, out_b, gain1, shift1, w_in, b_in, w_out, b_out, gain2, shift2 = params
    feats = low(fourier(box))
    start = low_back(hidden + matmul(feats, lay_w))
    start_low = low(start)
    qkv = matmul(start_low, qkv_w)
    query = low(low_back(qkv[:, :D] + qv_b[0]))
    keys = low(low_back(qkv[:, D:2 * D]))
    values = low(low_back(qkv[:, 2 * D:] + qv_b[1]))
    pos = jnp.arange(LEN, dtype=jnp.int32)
    across = box[0] + box[2]
    down = box[1] + box[3]
    bias = jnp.take(tables[0], level(pos[None, :] - pos[:, None], NEAR_EDGES), axis=0)
    bias = bias + jnp.take(tables[1], level(across[None, :] - across[:, None], FAR_EDGES), axis=0)
    bias = bias + jnp.take(tables[2], level(down[None, :] - down[:, None], FAR_EDGES), axis=0)
    bias = jnp.transpose(bias, (2, 0, 1))
    q3 = query.reshape(LEN, HEADS, HEAD_DIM)
    k3 = keys.reshape(LEN, HEADS, HEAD_DIM)
    v3 = values.reshape(LEN, HEADS, HEAD_DIM)
    scores = jnp.einsum('qhd,khd->hqk', q3, k3, precision=lax.Precision.HIGHEST) * 0.125 + bias
    scores = low_back(scores)
    valid = pos < length
    scores = jnp.where(valid[None, None, :], scores, -1e+30)
    top = lax.optimization_barrier(jnp.max(scores, axis=-1, keepdims=True))
    expo = jnp.exp(scores - top)
    probs = expo / lax.optimization_barrier(jnp.sum(expo, axis=-1, keepdims=True))
    context = jnp.einsum('hqk,khd->qhd', low(probs), v3, precision=lax.Precision.HIGHEST).reshape(LEN, D)
    context = low(low_back(context))
    attended = low_back(matmul(context, out_w) + out_b)
    mid = layer_norm(start + attended, gain1, shift1)
    inner = low_back(matmul(low(mid), w_in) + b_in)
    activated = low(jax.nn.gelu(inner, approximate=False))
    branch = low_back(matmul(activated, w_out) + b_out)
    return layer_norm(mid + branch, gain2, shift2)

def reference(hidden_in, boxes, lengths, cotangent, layout_weight, qkv_weight, qv_bias, bias_tables, out_weight, out_bias, norm1_gain, norm1_bias, ff_in, ff_in_bias, ff_out, ff_out_bias, norm2_gain, norm2_bias):
    params = tuple((p.astype(jnp.float32) for p in (layout_weight, qkv_weight, qv_bias, bias_tables, out_weight, out_bias, norm1_gain, norm1_bias, ff_in, ff_in_bias, ff_out, ff_out_bias, norm2_gain, norm2_bias)))
    group = math.gcd(NSEQ, max(1, 4096 // LEN))
    count = NSEQ // group
    inputs = hidden_in.astype(jnp.float32).reshape(count, group, LEN, D)
    upstreams = cotangent.astype(jnp.float32).reshape(count, group, LEN, D)
    box_groups = jnp.transpose(boxes.reshape(4, count, group, LEN), (1, 2, 0, 3))
    len_groups = lengths.reshape(count, group)

    def step(totals, item):
        hidden, upstream, box, length = item

        def run(hidden_val, param_val):
            return jax.vmap(layer, in_axes=(None, 0, 0, 0))(param_val, hidden_val, box, length)
        result, pull = jax.vjp(run, hidden, params)
        hidden_grad, param_grads = pull(upstream)
        totals = tuple((a + b for a, b in zip(totals, param_grads)))
        return (totals, (result.astype(jnp.bfloat16), hidden_grad.astype(jnp.bfloat16)))
    zeros = tuple((jnp.zeros_like(p) for p in params))
    grads, (outputs, in_grads) = lax.scan(step, zeros, (inputs, upstreams, box_groups, len_groups))
    lay_g, qkv_g, qvb_g, tab_g, outw_g, outb_g, gain1_g, shift1_g, ffin_g, ffinb_g, ffout_g, ffoutb_g, gain2_g, shift2_g = grads
    return (outputs.reshape(NSEQ, LEN, D), in_grads.reshape(NSEQ, LEN, D), lay_g, qkv_g, qvb_g, tab_g, outw_g, outb_g, gain1_g, shift1_g, ffin_g, ffinb_g, ffout_g, ffoutb_g, gain2_g, shift2_g)
```

```python
import functools, math
import numpy as np
import jax, jax.numpy as jnp
from jax import lax
from jax.experimental import pallas as pl
from jax.experimental.pallas import tpu as pltpu

BF=jnp.bfloat16; F32=jnp.float32
NEAR_EDGES = (1, 2, 3, 4, 5, 6, 7, 8, 12, 16, 24, 32, 64, 128, 256)
FAR_EDGES = (1, 2, 4, 8, 16, 32, 64, 96, 128, 192, 256, 384, 512, 768, 1024)
LOG2E=math.log2(math.e)
IB=256
JC=128

def nt(a,b):
    return lax.dot_general(a,b,(((1,),(1,)),((),())),preferred_element_type=F32)
def nn(a,b):
    return lax.dot_general(a,b,(((1,),(0,)),((),())),preferred_element_type=F32)
def level(rel, edges):
    magnitude = jnp.abs(rel)
    result = jnp.zeros(rel.shape, jnp.int32)
    for edge in edges:
        result = result + (magnitude >= edge).astype(jnp.int32)
    return result + 16 * (rel > 0).astype(jnp.int32)

def lookup(table, idx):
    rows=idx.shape[0]
    t=jnp.broadcast_to(table[0:1], (rows,128))
    return jnp.take_along_axis(t, idx, axis=1, mode="promise_in_bounds")

def far_level(d, lo, hi):
    a=jnp.abs(d)
    small=lookup(lo, jnp.minimum(a,127))
    big=lookup(hi, a>>4)
    return jnp.where(a<16, small, big)+jnp.where(d>0,16,0)

def fwd_kernel(len_ref, q_ref, k_ref, v_ref, cq_ref, ck_ref, lev_ref, tab_ref, nidx_ref,
               ctx_ref, p_ref, linv_ref, idx_ref, wide_ref, vt_ref, s_ref):
    g=pl.program_id(0); b=pl.program_id(1)
    full=k_ref.shape[0]
    nj=full//JC
    @pl.when(g==0)
    def _():
        length=len_ref[0]
        for m in range(nj):
            rows=slice(m*JC,(m+1)*JC)
            valid=(lax.broadcasted_iota(jnp.int32,(JC,128),0)+m*JC)<length
            for kind in range(2):
                ck=ck_ref[kind,rows,:]
                for c in range(IB//128):
                    d=ck-cq_ref[kind:kind+1,c*128:(c+1)*128]
                    idx=far_level(d,lev_ref[0:8],lev_ref[8:16])
                    if kind==0: idx=jnp.where(valid,idx,32)
                    idx_ref[kind,b,rows,c*128:(c+1)*128]=idx
    @pl.when(b==0)
    def _():
        vt_ref[0:128,:]=v_ref[...].T
        vt_ref[128:144,:]=jnp.ones((16,full),BF)
        for h in range(2):
            for c in range(2*full//128):
                wide_ref[h,:,c*128:(c+1)*128]=lookup(tab_ref[h,0],nidx_ref[:,c*128:(c+1)*128])
    lane=lax.broadcasted_iota(jnp.int32,(IB,128),1)
    q2=q_ref[...]*jnp.asarray(0.125,BF)
    outs=[]
    for h in range(2):
        qh=jnp.where((lane<64)==(h==0),q2,jnp.zeros_like(q2))
        top=jnp.full((8,IB),-jnp.inf,F32)
        for m in range(nj):
            rows=slice(m*JC,(m+1)*JC)
            s=nt(k_ref[rows,:],qh)
            near=wide_ref[h,:,pl.ds(pl.multiple_of(b*IB+(full-m*JC),128),IB)]
            bias=jnp.concatenate([lookup(tab_ref[h,1],idx_ref[0,b,rows,c*128:(c+1)*128])+lookup(tab_ref[h,2],idx_ref[1,b,rows,c*128:(c+1)*128]) for c in range(IB//128)],axis=1)
            s=s+near+bias
            s_ref[rows,:]=s
            top=jnp.maximum(top,jnp.max(s.reshape(JC//8,8,IB),axis=0))
        mx=jnp.max(top,axis=0,keepdims=True)*LOG2E
        for m in range(nj):
            rows=slice(m*JC,(m+1)*JC)
            p_ref[h,0,rows,:]=jnp.exp2(s_ref[rows,:]*LOG2E-mx).astype(BF)
        lhs=jnp.concatenate([vt_ref[64*h:64*h+64,:],vt_ref[128:144,:]],axis=0)
        r=nn(lhs,p_ref[h,0])
        inv=1.0/r[64:65]
        linv_ref[0,h:h+1,:]=inv
        outs.append(r[:64]*inv)
    ctx_ref[...]=jnp.concatenate(outs,axis=0).T.astype(BF)

def fwd_attention(q,k,v,qcol,kcol,vcol,length,crow,ccol,lev,tab,nidx,heads=12):
    full=q.shape[0]; width=heads*64; pairs=heads//2; nb=full//IB
    return pl.pallas_call(
        fwd_kernel, grid=(pairs,nb),
        in_specs=[pl.BlockSpec(memory_space=pltpu.SMEM),
          pl.BlockSpec((IB,128),lambda g,b:(b,qcol+g)),
          pl.BlockSpec((full,128),lambda g,b:(0,kcol+g)),
          pl.BlockSpec((full,128),lambda g,b:(0,vcol+g)),
          pl.BlockSpec((2,IB),lambda g,b:(0,b)),
          pl.BlockSpec((2,full,128),lambda g,b:(0,0,0)),
          pl.BlockSpec((16,128),lambda g,b:(0,0)),
          pl.BlockSpec((2,3,8,128),lambda g,b:(g,0,0,0)),
          pl.BlockSpec((128,2*full),lambda g,b:(0,0))],
        out_specs=[pl.BlockSpec((IB,128),lambda g,b:(b,g)),
          pl.BlockSpec((2,1,full,IB),lambda g,b:(g,b,0,0)),
          pl.BlockSpec((1,8,IB),lambda g,b:(g,0,b))],
        out_shape=[jax.ShapeDtypeStruct((full,width),BF),
          jax.ShapeDtypeStruct((heads,nb,full,IB),BF),
          jax.ShapeDtypeStruct((pairs,8,full),F32)],
        scratch_shapes=[pltpu.VMEM((2,nb,full,IB),jnp.int32),pltpu.VMEM((2,128,2*full),F32),
          pltpu.VMEM((144,full),BF),pltpu.VMEM((full,IB),F32)],
        compiler_params=pltpu.CompilerParams(vmem_limit_bytes=48*1024*1024),
        cost_estimate=pl.CostEstimate(flops=2*2*heads*full*full*64*4,bytes_accessed=heads*full*full*2,transcendentals=heads*full*full),
        name="attend",
    )(length,q,k,v,crow,ccol,lev,tab,nidx)

def bwd_kernel(q_ref,k_ref,v_ref,go_ref,ctx_ref,p_ref,linv_ref,
               dq_ref,dk_ref,dv_ref,ds_ref,diag_ref,
               kt_ref,acc_ref,wide_ref):
    g=pl.program_id(0); b=pl.program_id(1); nb=pl.num_programs(1)
    full=k_ref.shape[0]
    nj=full//JC
    @pl.when(b==0)
    def _():
        kt_ref[...]=k_ref[...].T
        acc_ref[...]=jnp.zeros_like(acc_ref)
        wide_ref[...]=jnp.zeros_like(wide_ref)
    gt=go_ref[...].astype(F32).T
    ct=ctx_ref[...].astype(F32).T
    rowi=lax.broadcasted_iota(jnp.int32,(128,IB),0)
    inv=jnp.where(rowi<64,jnp.broadcast_to(linv_ref[0,0:1,:],(128,IB)),jnp.broadcast_to(linv_ref[0,1:2,:],(128,IB)))
    gs=gt*inv
    pr=gs*ct
    gsb=gs.astype(BF)
    gos=gs.T.astype(BF)
    lane=lax.broadcasted_iota(jnp.int32,(IB,128),1)
    q2=q_ref[...]
    zero=jnp.zeros_like(q2)
    qs=[];gg=[];dqs=[]
    for h in range(2):
        keep=(lane<64)==(h==0)
        qs.append(jnp.where(keep,q2,zero)); gg.append(jnp.where(keep,gos,zero))
        dd=jnp.sum(pr[64*h:64*h+64],axis=0,keepdims=True)
        gh=jnp.where((rowi<64)==(h==0),gsb,jnp.zeros_like(gsb))
        for m in range(nj):
            rows=slice(m*JC,(m+1)*JC)
            gp=nn(v_ref[rows,:],gh)
            ds=p_ref[h,0,rows,:].astype(F32)*(gp-dd)
            ds_ref[h,0,rows,:]=ds.astype(BF)
            sl=pl.ds(pl.multiple_of(b*IB+(full-m*JC),128),IB)
            wide_ref[h,:,sl]=wide_ref[h,:,sl]+ds
        dqs.append(nn(kt_ref[64*h:64*h+64,:],ds_ref[h,0]))
    qcat=jnp.concatenate(qs,axis=0); gcat=jnp.concatenate(gg,axis=0)
    for m in range(nj):
        rows=slice(m*JC,(m+1)*JC)
        acc_ref[0,rows,:]+=nn(jnp.concatenate([ds_ref[0,0,rows,:],ds_ref[1,0,rows,:]],axis=1),qcat)
        acc_ref[1,rows,:]+=nn(jnp.concatenate([p_ref[0,0,rows,:],p_ref[1,0,rows,:]],axis=1),gcat)
    dq_ref[...]=(jnp.concatenate(dqs,axis=0)*0.125).T.astype(BF)
    @pl.when(b==nb-1)
    def _():
        dk_ref[...]=(acc_ref[0]*0.125).astype(BF)
        dv_ref[...]=acc_ref[1].astype(BF)
        for h in range(2):
            tot=jnp.zeros((8,2*full),F32)
            for r in range(16):
                x=wide_ref[h,r*8:(r+1)*8,:]
                tot=tot+pltpu.roll(x,2*full-r*8,1) if r else tot+x
            one=tot[0:1]
            for r in range(1,8):
                one=one+pltpu.roll(tot[r:r+1],2*full-r,1)
            diag_ref[0,h:h+1,:]=one

def bwd_attention(q,k,v,qcol,kcol,vcol,go,ctx,p,linv,heads=12):
    full=q.shape[0]; width=heads*64; pairs=heads//2; nb=full//IB
    return pl.pallas_call(
        bwd_kernel, grid=(pairs,nb),
        in_specs=[pl.BlockSpec((IB,128),lambda g,b:(b,qcol+g)),
          pl.BlockSpec((full,128),lambda g,b:(0,kcol+g)),
          pl.BlockSpec((full,128),lambda g,b:(0,vcol+g)),
          pl.BlockSpec((IB,128),lambda g,b:(b,g)),
          pl.BlockSpec((IB,128),lambda g,b:(b,g)),
          pl.BlockSpec((2,1,full,IB),lambda g,b:(g,b,0,0)),
          pl.BlockSpec((1,8,IB),lambda g,b:(g,0,b))],
        out_specs=[pl.BlockSpec((IB,128),lambda g,b:(b,g)),
          pl.BlockSpec((full,128),lambda g,b:(0,g)),
          pl.BlockSpec((full,128),lambda g,b:(0,g)),
          pl.BlockSpec((2,1,full,IB),lambda g,b:(g,b,0,0)),
          pl.BlockSpec((1,8,2*full),lambda g,b:(g,0,0))],
        out_shape=[jax.ShapeDtypeStruct((full,width),BF)]*3+[
          jax.ShapeDtypeStruct((heads,nb,full,IB),BF),
          jax.ShapeDtypeStruct((pairs,8,2*full),F32)],
        scratch_shapes=[pltpu.VMEM((128,full),BF),pltpu.VMEM((2,full,128),F32),pltpu.VMEM((2,128,2*full),F32)],
        compiler_params=pltpu.CompilerParams(vmem_limit_bytes=48*1024*1024),
        cost_estimate=pl.CostEstimate(flops=2*4*heads*full*full*64*4,bytes_accessed=2*heads*full*full*2,transcendentals=0),
        name="attend_back",
    )(q,k,v,go,ctx,p,linv)

THRESH=[-8192]+[1-e for e in reversed(FAR_EDGES)]+list(FAR_EDGES)
def hist_kernel(ds_ref, crow_ref, ccol_ref, out_ref, acc_ref, *, heads, dt):
    t=pl.program_id(0)
    nb=ds_ref.shape[1]
    sub=ds_ref.shape[2]//16
    @pl.when(t==0)
    def _(): acc_ref[...]=jnp.zeros_like(acc_ref)
    one=jnp.ones((16,IB),BF); zero=jnp.zeros((16,IB),BF)
    for u in range(sub):
        for kb in range(nb):
            parts=[]
            for kind in range(2):
                row=jnp.broadcast_to(crow_ref[kind:kind+1,kb*IB:(kb+1)*IB],(16,IB)).astype(dt)
                col=jnp.concatenate([ccol_ref[kind,u*16:(u+1)*16,:]]*(IB//128),axis=1)
                for e in range(32):
                    th=THRESH[min(e,30)]
                    parts.append(jnp.where(row<=(col-th).astype(dt),one,zero))
            lhs=jnp.concatenate(parts,axis=0)
            rhs=ds_ref[:,kb,u*16:(u+1)*16,:].reshape(heads*16,IB)
            acc_ref[...]+=nt(lhs,rhs)
    @pl.when(t==pl.num_programs(0)-1)
    def _():
        r=lax.broadcasted_iota(jnp.int32,(1024,heads*16),0); c=lax.broadcasted_iota(jnp.int32,(1024,heads*16),1)
        a=jnp.where((r%16)==(c%16),acc_ref[...],0.0)
        a=jnp.sum(a.reshape(64,16,heads*16),axis=1)
        out_ref[...]=a
def hist(ds,crow,ccol,heads=12,jb=32,dt=jnp.int32):
    nb,full=ds.shape[1:3]
    return pl.pallas_call(functools.partial(hist_kernel,heads=heads,dt=dt),grid=(full//jb,),
        in_specs=[pl.BlockSpec((heads,nb,jb,IB),lambda t:(0,0,t,0)),
          pl.BlockSpec((2,full),lambda t:(0,0)),
          pl.BlockSpec((2,jb,128),lambda t:(0,t,0))],
        out_specs=pl.BlockSpec((64,heads*16),lambda t:(0,0)),
        out_shape=jax.ShapeDtypeStruct((64,heads*16),F32),
        scratch_shapes=[pltpu.VMEM((1024,heads*16),F32)],
        compiler_params=pltpu.CompilerParams(vmem_limit_bytes=48*1024*1024),
        cost_estimate=pl.CostEstimate(flops=2*full*full*64*256,bytes_accessed=heads*full*full*2,transcendentals=0),
        name="bucket_sums")(ds,crow,ccol)

def tables(bias_tables, full):
    t=jnp.transpose(bias_tables.astype(F32),(2,0,1))
    t=jnp.pad(t,((0,0),(0,0),(0,96)))
    t=t.at[:,1,32].set(-1e30)
    return jnp.broadcast_to(t[:,:,None,:],(t.shape[0],3,8,128))
def np_level(d,edges):
    a=np.abs(d); r=np.zeros(d.shape,np.int32)
    for e in edges: r+=(a>=e)
    return r+16*(d>0)
def consts(full):
    lo=np_level(-np.arange(128),FAR_EDGES).astype(np.int32)
    hi=np_level(-np.arange(128)*16,FAR_EDGES).astype(np.int32)
    lev=np.concatenate([np.broadcast_to(lo,(8,128)),np.broadcast_to(hi,(8,128))])
    return jnp.asarray(lev)
def near_idx(full):
    r=lax.broadcasted_iota(jnp.int32,(128,2*full),0); u=lax.broadcasted_iota(jnp.int32,(128,2*full),1)
    return level(r+full-u,NEAR_EDGES)


from jax.sharding import PartitionSpec as P

BOXQ = 1000


def fourier(coords):
    scaled = coords.astype(F32) / BOXQ
    freqs = (jnp.arange(16, dtype=F32) + 1.0) * math.pi
    angle = scaled[:, :, None] * freqs[None, None, :]
    waves = jnp.concatenate([jnp.sin(angle), jnp.cos(angle)], axis=2)
    return jnp.transpose(waves, (1, 0, 2)).reshape(coords.shape[1], 128)


def layer_norm(resid, gain, shift):
    centre = resid - jnp.mean(resid, axis=-1, keepdims=True)
    spread = jnp.mean(centre * centre, axis=-1, keepdims=True)
    return centre * lax.rsqrt(spread + 1e-06) * gain + shift


def gelu_exact(value):
    return jax.nn.gelu(value, approximate=False)


def inner(left, right):
    return lax.dot_general(left, right, (((0,), (0,)), ((), ())), preferred_element_type=F32)


def far_table(sums):
    total = sums[0]
    count = len(FAR_EDGES)
    below = [total - sums[count - i] for i in range(count)]
    above = [sums[count + 1 + i] for i in range(count)]
    zero = jnp.zeros_like(total)
    rows = [total - below[0] - above[0]]
    for side in (below, above):
        edges = side + [zero]
        rows += [edges[i] - edges[i + 1] for i in range(count)]
        if side is below:
            rows.append(zero)
    return jnp.stack(rows)


def swap(part, me):
    own = jnp.where(me == 0, part[0], part[1])
    other = jnp.where(me == 0, part[1], part[0])
    came = lax.ppermute(other, "half", [(0, 1), (1, 0)])
    return jnp.concatenate([jnp.where(me == 0, own, came), jnp.where(me == 0, came, own)], axis=0)


def unswap(whole, me):
    rows = whole.shape[0] // 2
    own = jnp.where(me == 0, whole[:rows], whole[rows:])
    other = jnp.where(me == 0, whole[rows:], whole[:rows])
    came = lax.ppermute(other, "half", [(0, 1), (1, 0)])
    return jnp.stack([jnp.where(me == 0, own, came), jnp.where(me == 0, came, own)])


def shards(hidden_in, boxes, lengths, cotangent, layout_weight, qkv_weight, qv_bias, bias_tables, out_weight,
           out_bias, norm1_gain, norm1_bias, ff_in, ff_in_bias, ff_out, ff_out_bias, norm2_gain, norm2_bias):
    width = hidden_in.shape[2]
    full = boxes.shape[2]
    heads = bias_tables.shape[2]
    me = lax.axis_index("half")
    hidden = swap(hidden_in, me)
    box = lax.dynamic_index_in_dim(boxes, me, 1, keepdims=False)
    length = lax.dynamic_slice_in_dim(lengths, me, 1, 0)
    feats = fourier(box).astype(BF)
    start = hidden.astype(F32) + nn(feats, layout_weight)
    start_low = start.astype(BF)
    bias3 = jnp.concatenate([qv_bias[0], jnp.zeros_like(qv_bias[0]), qv_bias[1]]).astype(F32)
    qkv = (nn(start_low, qkv_weight) + bias3).astype(BF)
    crow = jnp.stack([box[0] + box[2], box[1] + box[3]])
    ccol = jnp.broadcast_to(crow[:, :, None], (2, full, 128))
    pairs = heads // 2
    context, probs, linv = fwd_attention(
        qkv, qkv, qkv, 0, pairs, 2 * pairs, length, crow, ccol, consts(full), tables(bias_tables, full),
        near_idx(full), heads)
    upstream = swap(cotangent, me).astype(F32)
    attended = nn(context, out_weight) + out_bias.astype(F32)
    mid, norm1_pull = jax.vjp(layer_norm, start + attended, norm1_gain.astype(F32), norm1_bias.astype(F32))
    mid_low = mid.astype(BF)
    hidden_pre = nn(mid_low, ff_in) + ff_in_bias.astype(F32)
    activated, gelu_pull = jax.vjp(gelu_exact, hidden_pre)
    activated = activated.astype(BF)
    branch = nn(activated, ff_out) + ff_out_bias.astype(F32)
    result, norm2_pull = jax.vjp(layer_norm, mid + branch, norm2_gain.astype(F32), norm2_bias.astype(F32))
    layer_out = unswap(result.astype(BF), me)
    grad_r2, gain2_grad, shift2_grad = norm2_pull(upstream)
    grad_ff = grad_r2.astype(BF)
    ffout_grad = inner(activated, grad_ff)
    ffoutb_grad = jnp.sum(grad_ff.astype(F32), axis=0)
    grad_inner = gelu_pull(nt(grad_ff, ff_out))[0].astype(BF)
    ffin_grad = inner(mid_low, grad_inner)
    ffinb_grad = jnp.sum(grad_inner.astype(F32), axis=0)
    grad_mid = grad_r2 + nt(grad_inner, ff_in)
    grad_r1, gain1_grad, shift1_grad = norm1_pull(grad_mid)
    grad_att = grad_r1.astype(BF)
    outw_grad = inner(context, grad_att)
    outb_grad = jnp.sum(grad_att.astype(F32), axis=0)
    grad_context = nt(grad_att, out_weight).astype(BF)
    grad_q, grad_k, grad_v, gscores, diag = bwd_attention(
        qkv, qkv, qkv, 0, pairs, 2 * pairs, grad_context, context, probs, linv, heads)
    grad_qkv = jnp.concatenate([grad_q, grad_k, grad_v], axis=1)
    qkv_grad = inner(start_low, grad_qkv)
    qvb_grad = jnp.stack([jnp.sum(grad_q.astype(F32), axis=0), jnp.sum(grad_v.astype(F32), axis=0)])
    grad_start = (grad_r1 + nt(grad_qkv, qkv_weight)).astype(BF)
    input_grad = unswap(grad_start, me)
    lay_grad = inner(feats, grad_start)
    sums = jnp.sum(hist(gscores, crow, ccol, heads, dt=jnp.int16).reshape(2, 32, heads, 16), axis=3)
    offset = lax.broadcasted_iota(jnp.int32, (2 * full, 32), 0)
    bucket = lax.broadcasted_iota(jnp.int32, (2 * full, 32), 1)
    near_hot = (level(full - offset, NEAR_EDGES) == bucket).astype(F32)
    diag = diag[:, :2].reshape(heads, 2 * full)
    near_grad = lax.dot_general(near_hot, diag, (((0,), (1,)), ((), ())), precision=lax.Precision.HIGHEST)
    table_grad = jnp.stack([near_grad, far_table(sums[0]), far_table(sums[1])])
    both = ("docs", "half")
    low = lambda x: x.astype(BF)
    ffout_total, ffin_total, outw_total = lax.psum((low(ffout_grad), low(ffin_grad), low(outw_grad)), both)
    qkv_total, lay_total = lax.psum((low(qkv_grad), low(lay_grad)), both)
    (qvb_total, table_total, outb_total, gain1_total, shift1_total, ffinb_total, ffoutb_total, gain2_total,
     shift2_total) = lax.psum((qvb_grad, table_grad, outb_grad, gain1_grad, shift1_grad, ffinb_grad, ffoutb_grad,
                               gain2_grad, shift2_grad), both)
    wide = lambda x: x.astype(F32)
    return (layer_out, input_grad, wide(lay_total), wide(qkv_total), qvb_total, table_total, wide(outw_total),
            outb_total, gain1_total, shift1_total, wide(ffin_total), ffinb_total, wide(ffout_total), ffoutb_total,
            gain2_total, shift2_total)


def solution(mesh):
    placed = (P("docs", "half", None), P(None, "docs", None), P("docs"), P("docs", "half", None)) + (P(),) * 14
    return jax.shard_map(
        shards, mesh=mesh, in_specs=placed,
        out_specs=(P("docs", "half", None), P("docs", "half", None)) + (P(),) * 14, check_vma=False)
```

```python
import functools, math
import numpy as np
import jax, jax.numpy as jnp
from jax import lax
from jax.experimental import pallas as pl
from jax.experimental.pallas import tpu as pltpu

BF=jnp.bfloat16; F32=jnp.float32
NEAR_EDGES = (1, 2, 3, 4, 5, 6, 7, 8, 12, 16, 24, 32, 64, 128, 256)
FAR_EDGES = (1, 2, 4, 8, 16, 32, 64, 96, 128, 192, 256, 384, 512, 768, 1024)
LOG2E=math.log2(math.e)
HISTF=15*10**9
IB=256
JC=128

def nt(a,b):
    return lax.dot_general(a,b,(((1,),(1,)),((),())),preferred_element_type=F32)
def nn(a,b):
    return lax.dot_general(a,b,(((1,),(0,)),((),())),preferred_element_type=F32)
def level(rel, edges):
    magnitude = jnp.abs(rel)
    result = jnp.zeros(rel.shape, jnp.int32)
    for edge in edges:
        result = result + (magnitude >= edge).astype(jnp.int32)
    return result + 16 * (rel > 0).astype(jnp.int32)

def lookup(table, idx):
    rows=idx.shape[0]
    t=jnp.broadcast_to(table[0:1], (rows,128))
    return jnp.take_along_axis(t, idx, axis=1, mode="promise_in_bounds")

UNIT=2048.0

def far_lane(d):
    a=jnp.abs(d)
    e=32-lax.clz(a)
    half=lax.shift_right_logical(a,jnp.maximum(e-2,0))&1
    return 2*e+half+jnp.where(d>0,32,0)

def fwd_kernel(len_ref, q_ref, k_ref, v_ref, cq_ref, ck_ref, tab_ref, nidx_ref,
               ctx_ref, p_ref, linv_ref, idx_ref, wide_ref, vt_ref, ka_ref, s0_ref, s1_ref, top_ref):
    t=pl.program_id(0)
    full=k_ref.shape[0]
    nj=full//JC; nb=full//IB
    last=pl.num_programs(0)-2
    now=jnp.minimum(t,last); before=jnp.maximum(t-1,0)
    g=now//nb; b=now%nb
    @pl.when(t<nb)
    def _():
        for m in range(nj):
            rows=slice(m*JC,(m+1)*JC)
            for c in range(IB//128):
                for kind in range(2):
                    idx_ref[kind,b,rows,c*128:(c+1)*128]=far_lane(ck_ref[kind,rows,:]-cq_ref[kind:kind+1,c*128:(c+1)*128])
    @pl.when(t==0)
    def _():
        key=lax.broadcasted_iota(jnp.int32,(full,128),0); lane=lax.broadcasted_iota(jnp.int32,(full,128),1)
        ka_ref[:,128:]=jnp.where((key>=len_ref[0])&(lane==0),-1e30,0.0).astype(BF)
        vt_ref[128:144,:]=jnp.ones((16,full),BF)
        s1_ref[...]=jnp.zeros_like(s1_ref)
        top_ref[...]=jnp.zeros_like(top_ref)
    @pl.when(b==0)
    def _():
        ka_ref[:,:128]=k_ref[...]
        for c in range(2*full//128):
            wide_ref[:,c*128:(c+1)*128]=lookup(tab_ref[0,0],nidx_ref[:,c*128:(c+1)*128])
    @pl.when(before%nb==0)
    def _():
        vt_ref[0:128,:]=v_ref[...].T
    scale=LOG2E/UNIT
    def body(cur_ref,prev_ref):
        rowi=lax.broadcasted_iota(jnp.int32,(128,IB),0)
        qt=(q_ref[...]*jnp.asarray(0.125*UNIT,BF)).T
        for h in range(2):
            qh=jnp.where((rowi<64)==(h==0),qt,jnp.zeros_like(qt))
            cur_ref[h]=nn(ka_ref[...],jnp.concatenate([qh,jnp.ones_like(qt)],axis=0))
        mx=[top_ref[h:h+1,:]*scale for h in range(2)]
        top=[jnp.full((8,IB),-jnp.inf,F32)]*2
        for m in range(nj):
            rows=slice(m*JC,(m+1)*JC)
            for h in range(2):
                p_ref[h,0,rows,:]=jnp.exp2(prev_ref[h,rows,:]*scale-mx[h]).astype(BF)
            x=wide_ref[:,pl.ds(pl.multiple_of(b*IB+(full-m*JC),128),IB)]
            x=x+jnp.concatenate([lookup(tab_ref[0,1],idx_ref[0,b,rows,c*128:(c+1)*128])+lookup(tab_ref[0,2],idx_ref[1,b,rows,c*128:(c+1)*128]) for c in range(IB//128)],axis=1)
            for h in range(2):
                y=(x&0xffff) if h==0 else lax.shift_right_logical(x,16)
                s=cur_ref[h,rows,:]+y.astype(F32)
                cur_ref[h,rows,:]=s
                top[h]=jnp.maximum(top[h],jnp.max(s.reshape(JC//8,8,IB),axis=0))
        for h in range(2):
            top_ref[h:h+1,:]=jnp.max(top[h],axis=0,keepdims=True)
        outs=[]
        for h in range(2):
            lhs=jnp.concatenate([vt_ref[64*h:64*h+64,:],vt_ref[128:144,:]],axis=0)
            r=nn(lhs,p_ref[h,0])
            inv=1.0/r[64:65]
            linv_ref[0,h:h+1,:]=inv
            outs.append(r[:64]*inv)
        ctx_ref[...]=jnp.concatenate(outs,axis=0).T.astype(BF)
    @pl.when(t%2==0)
    def _(): body(s0_ref,s1_ref)
    @pl.when(t%2==1)
    def _(): body(s1_ref,s0_ref)

def fwd_attention(q,k,v,qcol,kcol,vcol,length,crow,ccol,tab,nidx,heads=12):
    full=q.shape[0]; width=heads*64; pairs=heads//2; nb=full//IB; last=pairs*nb-1
    now=lambda t: jnp.minimum(t,last)
    was=lambda t: jnp.maximum(t-1,0)
    return pl.pallas_call(
        fwd_kernel, grid=(pairs*nb+1,),
        in_specs=[pl.BlockSpec(memory_space=pltpu.SMEM),
          pl.BlockSpec((IB,128),lambda t:(now(t)%nb,qcol+now(t)//nb)),
          pl.BlockSpec((full,128),lambda t:(0,kcol+now(t)//nb)),
          pl.BlockSpec((full,128),lambda t:(0,vcol+was(t)//nb)),
          pl.BlockSpec((2,IB),lambda t:(0,now(t)%nb)),
          pl.BlockSpec((2,full,128),lambda t:(0,0,0)),
          pl.BlockSpec((1,3,8,128),lambda t:(now(t)//nb,0,0,0)),
          pl.BlockSpec((128,2*full),lambda t:(0,0))],
        out_specs=[pl.BlockSpec((IB,128),lambda t:(was(t)%nb,was(t)//nb)),
          pl.BlockSpec((2,1,full,IB),lambda t:(was(t)//nb,was(t)%nb,0,0)),
          pl.BlockSpec((1,8,IB),lambda t:(was(t)//nb,0,was(t)%nb))],
        out_shape=[jax.ShapeDtypeStruct((full,width),BF),
          jax.ShapeDtypeStruct((heads,nb,full,IB),BF),
          jax.ShapeDtypeStruct((pairs,8,full),F32)],
        scratch_shapes=[pltpu.VMEM((2,nb,full,IB),jnp.int32),pltpu.VMEM((128,2*full),jnp.int32),
          pltpu.VMEM((144,full),BF),pltpu.VMEM((full,256),BF),pltpu.VMEM((2,full,IB),F32),pltpu.VMEM((2,full,IB),F32),
          pltpu.VMEM((8,IB),F32)],
        compiler_params=pltpu.CompilerParams(vmem_limit_bytes=48*1024*1024),
        cost_estimate=pl.CostEstimate(flops=1000,bytes_accessed=1000,transcendentals=0),
        name="attend",
    )(length,q,k,v,crow,ccol,tab,nidx)

def bwd_kernel(q_ref,k_ref,v_ref,go_ref,ctx_ref,p_ref,linv_ref,
               g3_ref,ds_ref,diag_ref,
               kt_ref,acc_ref,wide_ref,gp_ref):
    g=pl.program_id(0); b=pl.program_id(1); nb=pl.num_programs(1)
    full=k_ref.shape[0]
    nj=full//JC
    @pl.when(b==0)
    def _():
        kt_ref[...]=k_ref[...].T
        acc_ref[...]=jnp.zeros_like(acc_ref)
        wide_ref[...]=jnp.zeros_like(wide_ref)
    gt=go_ref[...].astype(F32).T
    ct=ctx_ref[...].astype(F32).T
    rowi=lax.broadcasted_iota(jnp.int32,(128,IB),0)
    inv=jnp.where(rowi<64,jnp.broadcast_to(linv_ref[0,0:1,:],(128,IB)),jnp.broadcast_to(linv_ref[0,1:2,:],(128,IB)))
    gs=gt*inv
    pr=gs*ct
    gsb=gs.astype(BF)
    gos=gs.T.astype(BF)
    lane=lax.broadcasted_iota(jnp.int32,(IB,128),1)
    q2=q_ref[...]
    zero=jnp.zeros_like(q2)
    qs=[];gg=[];dqs=[];dds=[]
    for h in range(2):
        keep=(lane<64)==(h==0)
        qs.append(jnp.where(keep,q2,zero)); gg.append(jnp.where(keep,gos,zero))
        dd=jnp.sum(pr[64*h:64*h+64],axis=0,keepdims=True)
        gh=jnp.where((rowi<64)==(h==0),gsb,jnp.zeros_like(gsb))
        gp_ref[h]=nn(v_ref[...],gh)
        dds.append(dd)
    for h in range(2):
        for m in range(nj):
            rows=slice(m*JC,(m+1)*JC)
            ds=p_ref[h,0,rows,:].astype(F32)*(gp_ref[h,rows,:]-dds[h])
            ds_ref[h,0,rows,:]=ds.astype(BF)
            sl=pl.ds(pl.multiple_of(b*IB+(full-m*JC),128),IB)
            wide_ref[h,:,sl]=wide_ref[h,:,sl]+ds
        dqs.append(nn(kt_ref[64*h:64*h+64,:],ds_ref[h,0]))
    qcat=jnp.concatenate(qs,axis=0); gcat=jnp.concatenate(gg,axis=0)
    acc_ref[0]+=nn(jnp.concatenate([ds_ref[0,0],ds_ref[1,0]],axis=1),qcat)
    acc_ref[1]+=nn(jnp.concatenate([p_ref[0,0],p_ref[1,0]],axis=1),gcat)
    g3_ref[0,pl.ds(pl.multiple_of(b*IB,IB),IB),:]=(jnp.concatenate(dqs,axis=0)*0.125).T.astype(BF)
    @pl.when(b==nb-1)
    def _():
        g3_ref[1]=(acc_ref[0]*0.125).astype(BF)
        g3_ref[2]=acc_ref[1].astype(BF)
        for h in range(2):
            tot=jnp.zeros((8,2*full),F32)
            for r in range(16):
                x=wide_ref[h,r*8:(r+1)*8,:]
                tot=tot+pltpu.roll(x,2*full-r*8,1) if r else tot+x
            one=tot[0:1]
            for r in range(1,8):
                one=one+pltpu.roll(tot[r:r+1],2*full-r,1)
            diag_ref[0,h:h+1,:]=one

def bwd_attention(q,k,v,qcol,kcol,vcol,go,ctx,p,linv,heads=12):
    full=q.shape[0]; width=heads*64; pairs=heads//2; nb=full//IB
    return pl.pallas_call(
        bwd_kernel, grid=(pairs,nb),
        in_specs=[pl.BlockSpec((IB,128),lambda g,b:(b,qcol+g)),
          pl.BlockSpec((full,128),lambda g,b:(0,kcol+g)),
          pl.BlockSpec((full,128),lambda g,b:(0,vcol+g)),
          pl.BlockSpec((IB,128),lambda g,b:(b,g)),
          pl.BlockSpec((IB,128),lambda g,b:(b,g)),
          pl.BlockSpec((2,1,full,IB),lambda g,b:(g,b,0,0)),
          pl.BlockSpec((1,8,IB),lambda g,b:(g,0,b))],
        out_specs=[pl.BlockSpec((3,full,128),lambda g,b:(0,0,g)),
          pl.BlockSpec((2,1,full,IB),lambda g,b:(g,b,0,0)),
          pl.BlockSpec((1,8,2*full),lambda g,b:(g,0,0))],
        out_shape=[jax.ShapeDtypeStruct((3,full,width),BF),
          jax.ShapeDtypeStruct((heads,nb,full,IB),BF),
          jax.ShapeDtypeStruct((pairs,8,2*full),F32)],
        scratch_shapes=[pltpu.VMEM((128,full),BF),pltpu.VMEM((2,full,128),F32),pltpu.VMEM((2,128,2*full),F32),pltpu.VMEM((2,full,IB),F32)],
        compiler_params=pltpu.CompilerParams(vmem_limit_bytes=48*1024*1024),
        cost_estimate=pl.CostEstimate(flops=1000,bytes_accessed=1000,transcendentals=0),
        input_output_aliases={5:1}, name="attend_back",
    )(q,k,v,go,ctx,p,linv)

THRESH=[-8192]+[1-e for e in reversed(FAR_EDGES)]+list(FAR_EDGES)
def hist_kernel(ds_ref, crow_ref, ccol_ref, out_ref, acc_ref, *, heads, dt):
    t=pl.program_id(0)
    nb=ds_ref.shape[1]
    sub=ds_ref.shape[2]//16
    @pl.when(t==0)
    def _(): acc_ref[...]=jnp.zeros_like(acc_ref)
    one=jnp.ones((16,IB),BF); zero=jnp.zeros((16,IB),BF)
    for u in range(sub):
        for kb in range(nb):
            parts=[]
            for kind in range(2):
                row=jnp.broadcast_to(crow_ref[kind:kind+1,kb*IB:(kb+1)*IB],(16,IB)).astype(dt)
                col=jnp.concatenate([ccol_ref[kind,u*16:(u+1)*16,:]]*(IB//128),axis=1)
                for e in range(32):
                    th=THRESH[min(e,30)]
                    parts.append(jnp.where(row<=(col-th).astype(dt),one,zero))
            lhs=jnp.concatenate(parts,axis=0)
            rhs=ds_ref[:,kb,u*16:(u+1)*16,:].reshape(heads*16,IB)
            acc_ref[...]+=nt(lhs,rhs)
    @pl.when(t==pl.num_programs(0)-1)
    def _():
        r=lax.broadcasted_iota(jnp.int32,(1024,heads*16),0); c=lax.broadcasted_iota(jnp.int32,(1024,heads*16),1)
        a=jnp.where((r%16)==(c%16),acc_ref[...],0.0)
        a=jnp.sum(a.reshape(64,16,heads*16),axis=1)
        out_ref[...]=a
def hist(ds,crow,ccol,heads=12,jb=32,dt=jnp.int32,part=0,parts=1):
    nb,full=ds.shape[1:3]; steps=full//jb//parts; at=part*steps
    return pl.pallas_call(functools.partial(hist_kernel,heads=heads,dt=dt),grid=(steps,),
        in_specs=[pl.BlockSpec((heads,nb,jb,IB),lambda t:(0,0,t+at,0)),
          pl.BlockSpec((2,full),lambda t:(0,0)),
          pl.BlockSpec((2,jb,128),lambda t:(0,t+at,0))],
        out_specs=pl.BlockSpec((64,heads*16),lambda t:(0,0)),
        out_shape=jax.ShapeDtypeStruct((64,heads*16),F32),
        scratch_shapes=[pltpu.VMEM((1024,heads*16),F32)],
        compiler_params=pltpu.CompilerParams(vmem_limit_bytes=48*1024*1024),
        cost_estimate=pl.CostEstimate(flops=HISTF,bytes_accessed=1000,transcendentals=0),
        name="bucket_sums")(ds,crow,ccol)

def np_level(d,edges):
    a=np.abs(d); r=np.zeros(d.shape,np.int32)
    for e in edges: r+=(a>=e)
    return r+16*(d>0)
def lanes_of():
    lane=np.arange(128)
    e=(lane%32)//2; half=lane%2
    a=np.where(e==0,0,np.where(e==1,1,2**np.maximum(e-1,0)+half*2**np.maximum(e-2,0)))
    return np_level(np.where((lane//32)%2==1,a,-a),FAR_EDGES)
def tables(bias_tables):
    near=np.arange(128)%32; far=lanes_of()
    hot=np.stack([near,far,far])[:,:,None]==np.arange(32)
    t=jnp.einsum('klb,kbh->hkl',jnp.asarray(hot,BF),bias_tables,preferred_element_type=F32)
    t=jnp.round((t+4.0)*UNIT).astype(jnp.int32)
    t=t[0::2]+(t[1::2]<<16)
    return jnp.broadcast_to(t[:,:,None,:],(t.shape[0],3,8,128))
def near_idx(full):
    r=lax.broadcasted_iota(jnp.int32,(128,2*full),0); u=lax.broadcasted_iota(jnp.int32,(128,2*full),1)
    return level(r+full-u,NEAR_EDGES)


from jax.sharding import PartitionSpec as P

BOXQ = 1000
BOTH = ("docs", "half")
TIE = -1


def fourier(coords):
    scaled = coords.astype(F32) / BOXQ
    freqs = (jnp.arange(16, dtype=F32) + 1.0) * math.pi
    angle = scaled[:, :, None] * freqs[None, None, :]
    waves = jnp.concatenate([jnp.sin(angle), jnp.cos(angle)], axis=2)
    return jnp.transpose(waves, (1, 0, 2)).reshape(coords.shape[1], 128)


def layer_norm(resid, gain, shift):
    centre = resid - jnp.mean(resid, axis=-1, keepdims=True)
    spread = jnp.mean(centre * centre, axis=-1, keepdims=True)
    return centre * lax.rsqrt(spread + 1e-06) * gain + shift


def gelu_pair(x):
    bell = jnp.exp2(x * x * (-0.5 * LOG2E))
    t = 1.0 / (1.0 + (0.3275911 * math.sqrt(0.5)) * jnp.abs(x))
    poly = t * (0.254829592 + t * (-0.284496736 + t * (1.421413741 + t * (-1.453152027 + t * 1.061405429))))
    tail = 0.5 * poly * bell
    cdf = jnp.where(x < 0, tail, 1.0 - tail)
    return x * cdf, cdf + x * bell * (1.0 / math.sqrt(2.0 * math.pi))


def inner(left, right):
    return lax.dot_general(left, right, (((0,), (0,)), ((), ())), preferred_element_type=F32)


def far_table(sums):
    total = sums[0]
    count = len(FAR_EDGES)
    below = [total - sums[count - i] for i in range(count)]
    above = [sums[count + 1 + i] for i in range(count)]
    zero = jnp.zeros_like(total)
    rows = [total - below[0] - above[0]]
    for side in (below, above):
        edges = side + [zero]
        rows += [edges[i] - edges[i + 1] for i in range(count)]
        if side is below:
            rows.append(zero)
    return jnp.stack(rows)


def swap(part, me):
    own = jnp.where(me == 0, part[0], part[1])
    other = jnp.where(me == 0, part[1], part[0])
    came = lax.ppermute(other, "half", [(0, 1), (1, 0)])
    return jnp.concatenate([jnp.where(me == 0, own, came), jnp.where(me == 0, came, own)], axis=0)


def unswap(whole, me):
    rows = whole.shape[0] // 2
    own = jnp.where(me == 0, whole[:rows], whole[rows:])
    other = jnp.where(me == 0, whole[rows:], whole[:rows])
    came = lax.ppermute(other, "half", [(0, 1), (1, 0)])
    return jnp.stack([jnp.where(me == 0, own, came), jnp.where(me == 0, came, own)])


class Route:
    def __init__(self):
        docs = lax.axis_size("docs")
        bits = [("docs", 1 << i) for i in range(docs.bit_length() - 1)]
        self.core = bits[0]
        y = ("half", 1)
        self.orders = [bits[1:2] + [y] + bits[2:], [y] + bits[1:], bits[2:] + bits[1:2] + [y]]
        self.all = bits + [y]
        self.pieces = docs * 2 // 2

    def mine(self, step):
        return (lax.axis_index(step[0]) // step[1]) % 2

    def move(self, x, step):
        axis, bit = step
        return lax.ppermute(x, axis, [(i, i ^ bit) for i in range(lax.axis_size(axis))])

    def product(self, left, right):
        mine = self.mine(self.core)
        cols = left.shape[1] // 2
        dot = lambda at: jnp.einsum("td,...tf->...df", lax.dynamic_slice_in_dim(left, at * cols, cols, 1), right,
                                    preferred_element_type=F32)
        send = dot(1 - mine).astype(BF)
        keep = dot(mine)
        return (keep + self.move(send, self.core).astype(F32)).astype(BF)

    def scatter(self, x, step):
        mine = self.mine(step)
        half = x.shape[0] // 2
        send = lax.dynamic_slice_in_dim(x, (1 - mine) * half, half, 0)
        keep = lax.dynamic_slice_in_dim(x, mine * half, half, 0)
        return (keep.astype(F32) + self.move(send, step).astype(F32)).astype(BF)

    def gather(self, x, step):
        mine = self.mine(step)
        came = self.move(x, step)
        return jnp.concatenate([jnp.where(mine == 0, x, came), jnp.where(mine == 0, came, x)], axis=0)

    def total(self, parts, between=None, tie=None):
        rows = [p.shape[0] // self.pieces for p in parts]
        x = jnp.concatenate([p.reshape(self.pieces, r, p.shape[1]) for p, r in zip(parts, rows)], axis=1)
        count = x.shape[1]
        x = jnp.pad(x, ((0, 0), (0, -count % 16), (0, 0)))
        cut = x.shape[1] // 2
        lanes = [x[:, :cut], x[:, cut:]]
        for i in range(len(self.orders[0])):
            if between and i < 4:
                lanes = between(i, 4, lanes)
            lanes = [self.scatter(x, order[i]) for x, order in zip(lanes, self.orders)]
        for i in reversed(range(len(self.orders[0]))):
            if tie and i == TIE:
                lanes = tie(lanes)
            lanes = [self.gather(x, order[i]) for x, order in zip(lanes, self.orders)]
        came = [self.move(x, self.core) for x in lanes]
        mine = self.mine(self.core)
        own, came = jnp.concatenate(lanes, axis=1), jnp.concatenate(came, axis=1)
        whole = jnp.concatenate([jnp.where(mine == 0, own, came), jnp.where(mine == 0, came, own)], axis=0)
        out = []
        at = 0
        for p, r in zip(parts, rows):
            out.append(whole[:, at:at + r].reshape(-1, p.shape[1]).astype(F32))
            at += r
        return out

    def small(self, parts):
        sizes = [p.size for p in parts]
        flat = jnp.concatenate([p.reshape(-1) for p in parts])
        count = flat.shape[0]
        flat = jnp.pad(flat, (0, -count % 1024)).reshape(-1, 128)
        for step in self.all:
            flat = flat + self.move(flat, step)
        flat = flat.reshape(-1)
        out = []
        at = 0
        for p, n in zip(parts, sizes):
            out.append(flat[at:at + n].reshape(p.shape))
            at += n
        return out


def shards(hidden_in, boxes, lengths, cotangent, layout_weight, qkv_weight, qv_bias, bias_tables, out_weight,
           out_bias, norm1_gain, norm1_bias, ff_in, ff_in_bias, ff_out, ff_out_bias, norm2_gain, norm2_bias):
    width = hidden_in.shape[2]
    full = boxes.shape[2]
    heads = bias_tables.shape[2]
    me = lax.axis_index("half")
    route = Route()
    hidden = swap(hidden_in, me)
    box = lax.dynamic_index_in_dim(boxes, me, 1, keepdims=False)
    length = lax.dynamic_slice_in_dim(lengths, me, 1, 0)
    feats = fourier(box).astype(BF)
    start = hidden.astype(F32) + nn(feats, layout_weight)
    start_low = start.astype(BF)
    bias3 = jnp.concatenate([qv_bias[0], jnp.zeros_like(qv_bias[0]), qv_bias[1]]).astype(F32)
    qkv = (nn(start_low, qkv_weight) + bias3).astype(BF)
    crow = jnp.stack([box[0] + box[2], box[1] + box[3]])
    ccol = jnp.broadcast_to(crow[:, :, None], (2, full, 128))
    pairs = heads // 2
    context, probs, linv = fwd_attention(
        qkv, qkv, qkv, 0, pairs, 2 * pairs, length, crow, ccol, tables(bias_tables), near_idx(full), heads)
    upstream = swap(cotangent, me).astype(F32)
    attended = nn(context, out_weight) + out_bias.astype(F32)
    mid, norm1_pull = jax.vjp(layer_norm, start + attended, norm1_gain.astype(F32), norm1_bias.astype(F32))
    mid_low = mid.astype(BF)
    hidden_pre = nn(mid_low, ff_in) + ff_in_bias.astype(F32)
    activated, slope = gelu_pair(hidden_pre)
    activated = activated.astype(BF)
    slope = slope.astype(BF)
    branch = nn(activated, ff_out) + ff_out_bias.astype(F32)
    result, norm2_pull = jax.vjp(layer_norm, mid + branch, norm2_gain.astype(F32), norm2_bias.astype(F32))
    layer_out = unswap(result.astype(BF), me)
    grad_r2, gain2_grad, shift2_grad = norm2_pull(upstream)
    grad_ff = grad_r2.astype(BF)
    ffout_part = inner(activated, grad_ff).astype(BF)
    ffoutb_grad = jnp.sum(grad_ff.astype(F32), axis=0)
    grad_inner = (nt(grad_ff, ff_out) * slope.astype(F32)).astype(BF)
    ffin_part = inner(mid_low, grad_inner).astype(BF)
    ffinb_grad = jnp.sum(grad_inner.astype(F32), axis=0)
    grad_mid = grad_r2 + nt(grad_inner, ff_in)
    grad_r1, gain1_grad, shift1_grad = norm1_pull(grad_mid)
    grad_att = grad_r1.astype(BF)
    outw_part = inner(context, grad_att).astype(BF)
    outb_grad = jnp.sum(grad_att.astype(F32), axis=0)
    grad_context = nt(grad_att, out_weight).astype(BF)
    early = jnp.concatenate([ffout_part] + [ffin_part[:, c * width:(c + 1) * width] for c in range(ffin_part.shape[1] // width)] + [outw_part], axis=0)
    grad_context = lax.optimization_barrier((early, grad_context))[1]
    early = lax.psum(early, BOTH)
    grad3, gscores, diag = bwd_attention(
        qkv, qkv, qkv, 0, pairs, 2 * pairs, grad_context, context, probs, linv, heads)
    qkv_part = route.product(start_low, grad3)
    qvb_grad = jnp.sum(grad3.astype(F32), axis=1)[0::2]
    grad_start = (grad_r1 + sum(nt(grad3[c], qkv_weight[:, c * width:(c + 1) * width]) for c in range(3))).astype(BF)
    input_grad = unswap(grad_start, me)
    lay_part = route.product(feats, grad_start)
    bucket_parts = []

    def between(i, count, lanes):
        row = crow
        if i:
            row, *lanes = lax.optimization_barrier((crow, *lanes))
        bucket_parts.append(hist(gscores, row, ccol, heads, dt=jnp.int16, part=i, parts=count))
        return lanes

    held = [early]

    def tie(lanes):
        held[0], *lanes = lax.optimization_barrier((held[0], *lanes))
        return lanes

    groups = route.total([qkv_part[0], qkv_part[1], qkv_part[2], lay_part], between, tie)
    early = held[0]
    sums = jnp.sum(sum(bucket_parts).reshape(2, 32, heads, 16), axis=3)
    offset = lax.broadcasted_iota(jnp.int32, (2 * full, 32), 0)
    bucket = lax.broadcasted_iota(jnp.int32, (2 * full, 32), 1)
    near_hot = (level(full - offset, NEAR_EDGES) == bucket).astype(F32)
    diag = diag[:, :2].reshape(heads, 2 * full)
    near_grad = lax.dot_general(near_hot, diag, (((0,), (1,)), ((), ())), precision=lax.Precision.HIGHEST)
    table_grad = jnp.stack([near_grad, far_table(sums[0]), far_table(sums[1])])

    qkv_total = jnp.concatenate(groups[:3], axis=1)
    lay_total = groups[3]
    (ffinb_total, ffoutb_total, gain2_total, shift2_total, outb_total, gain1_total, shift1_total, qvb_total,
     table_total) = route.small([ffinb_grad, ffoutb_grad, gain2_grad, shift2_grad, outb_grad, gain1_grad, shift1_grad,
                                 qvb_grad, table_grad])
    ff = ffin_part.shape[1]
    ffout_total = early[:ff].astype(F32)
    ffin_total = jnp.concatenate([early[ff + c * width:ff + (c + 1) * width] for c in range(ff // width)], axis=1).astype(F32)
    outw_total = early[2 * ff:].astype(F32)
    return (layer_out, input_grad, lay_total, qkv_total, qvb_total, table_total, outw_total,
            outb_total, gain1_total, shift1_total, ffin_total, ffinb_total, ffout_total, ffoutb_total,
            gain2_total, shift2_total)


def solution(mesh):
    placed = (P("docs", "half", None), P(None, "docs", None), P("docs"), P("docs", "half", None)) + (P(),) * 14
    return jax.shard_map(
        shards, mesh=mesh, in_specs=placed,
        out_specs=(P("docs", "half", None), P("docs", "half", None)) + (P(),) * 14, check_vma=False)
```

```python
import functools, math
import numpy as np
import jax, jax.numpy as jnp
from jax import lax
from jax.experimental import pallas as pl
from jax.experimental.pallas import tpu as pltpu

BF=jnp.bfloat16; F32=jnp.float32
NEAR_EDGES = (1, 2, 3, 4, 5, 6, 7, 8, 12, 16, 24, 32, 64, 128, 256)
FAR_EDGES = (1, 2, 4, 8, 16, 32, 64, 96, 128, 192, 256, 384, 512, 768, 1024)
LOG2E=math.log2(math.e)
HISTF=15*10**9
IB=256
FC=256
JC=128

def nt(a,b):
    return lax.dot_general(a,b,(((1,),(1,)),((),())),preferred_element_type=F32)
def nn(a,b):
    return lax.dot_general(a,b,(((1,),(0,)),((),())),preferred_element_type=F32)
def level(rel, edges):
    magnitude = jnp.abs(rel)
    result = jnp.zeros(rel.shape, jnp.int32)
    for edge in edges:
        result = result + (magnitude >= edge).astype(jnp.int32)
    return result + 16 * (rel > 0).astype(jnp.int32)

def lookup(table, idx):
    rows=idx.shape[0]
    t=jnp.broadcast_to(table[0:1], (rows,128))
    return jnp.take_along_axis(t, idx, axis=1, mode="promise_in_bounds")

UNIT=2048.0

def far_lane(d):
    a=jnp.abs(d)
    e=32-lax.clz(a)
    half=lax.shift_right_logical(a,jnp.maximum(e-2,0))&1
    return 2*e+half+jnp.where(d>0,32,0)

def fwd_kernel(len_ref, q_ref, k_ref, v_ref, cq_ref, ck_ref, tab_ref, nidx_ref,
               ctx_ref, p_ref, linv_ref, idx_ref, wide_ref, vt_ref, ka_ref, s0_ref, s1_ref, top_ref):
    t=pl.program_id(0)
    full=k_ref.shape[0]
    nj=full//JC; nb=full//IB
    last=pl.num_programs(0)-2
    now=jnp.minimum(t,last); before=jnp.maximum(t-1,0)
    g=now//nb; b=now%nb
    @pl.when(t<nb)
    def _():
        for m in range(nj):
            rows=slice(m*JC,(m+1)*JC)
            for c in range(IB//128):
                for kind in range(2):
                    idx_ref[kind,b,rows,c*128:(c+1)*128]=far_lane(ck_ref[kind,rows,:]-cq_ref[kind:kind+1,c*128:(c+1)*128])+64*kind
    @pl.when(t==0)
    def _():
        key=lax.broadcasted_iota(jnp.int32,(full,128),0); lane=lax.broadcasted_iota(jnp.int32,(full,128),1)
        ka_ref[:,128:]=jnp.where((key>=len_ref[0])&(lane==0),-1e30,0.0).astype(BF)
        vt_ref[128:144,:]=jnp.ones((16,full),BF)
        s1_ref[...]=jnp.zeros_like(s1_ref)
        top_ref[...]=jnp.zeros_like(top_ref)
    @pl.when(b==0)
    def _():
        ka_ref[:,:128]=k_ref[...]
        for c in range(2*full//128):
            wide_ref[:,c*128:(c+1)*128]=lookup(tab_ref[0,0],nidx_ref[:,c*128:(c+1)*128])
    @pl.when(before%nb==0)
    def _():
        vt_ref[0:128,:]=v_ref[...].T
    scale=LOG2E/UNIT
    def body(cur_ref,prev_ref):
        rowi=lax.broadcasted_iota(jnp.int32,(128,IB),0)
        qt=(q_ref[...]*jnp.asarray(0.125*UNIT,BF)).T
        qh=[jnp.concatenate([jnp.where((rowi<64)==(h==0),qt,jnp.zeros_like(qt)),jnp.ones_like(qt)],axis=0) for h in range(2)]
        mx=[top_ref[h:h+1,:]*scale for h in range(2)]
        top=[jnp.full((8,IB),-jnp.inf,F32)]*2
        lhs=[jnp.concatenate([vt_ref[64*h:64*h+64,:],vt_ref[128:144,:]],axis=0) for h in range(2)]
        acc=[jnp.zeros((80,IB),F32)]*2
        for m in range(full//FC):
            rows=slice(m*FC,(m+1)*FC)
            raw=[nn(ka_ref[rows,:],qh[h]) for h in range(2)]
            for h in range(2):
                p=jnp.exp2(prev_ref[h,rows,:]*scale-mx[h]).astype(BF)
                p_ref[h,0,rows,:]=p
                acc[h]=acc[h]+nn(lhs[h][:,rows],p)
            near=jnp.concatenate([wide_ref[:,pl.ds(pl.multiple_of(b*IB+(full-w*JC),128),IB)] for w in range(m*FC//JC,(m+1)*FC//JC)],axis=0)
            x=near+jnp.concatenate([lookup(tab_ref[0,1],idx_ref[0,b,rows,c*128:(c+1)*128])+lookup(tab_ref[0,1],idx_ref[1,b,rows,c*128:(c+1)*128]) for c in range(IB//128)],axis=1)
            for h in range(2):
                y=(x&0xffff) if h==0 else lax.shift_right_logical(x,16)
                s=raw[h]+y.astype(F32)
                cur_ref[h,rows,:]=s
                top[h]=jnp.maximum(top[h],jnp.max(s.reshape(FC//8,8,IB),axis=0))
        outs=[]
        for h in range(2):
            top_ref[h:h+1,:]=jnp.max(top[h],axis=0,keepdims=True)
            inv=1.0/acc[h][64:65]
            linv_ref[0,h:h+1,:]=inv
            outs.append(acc[h][:64]*inv)
        ctx_ref[...]=jnp.concatenate(outs,axis=0).T.astype(BF)
    @pl.when(t%2==0)
    def _(): body(s0_ref,s1_ref)
    @pl.when(t%2==1)
    def _(): body(s1_ref,s0_ref)

def fwd_attention(q,k,v,qcol,kcol,vcol,length,crow,ccol,tab,nidx,heads=12):
    full=q.shape[0]; width=heads*64; pairs=heads//2; nb=full//IB; last=pairs*nb-1
    now=lambda t: jnp.minimum(t,last)
    was=lambda t: jnp.maximum(t-1,0)
    return pl.pallas_call(
        fwd_kernel, grid=(pairs*nb+1,),
        in_specs=[pl.BlockSpec(memory_space=pltpu.SMEM),
          pl.BlockSpec((IB,128),lambda t:(now(t)%nb,qcol+now(t)//nb)),
          pl.BlockSpec((full,128),lambda t:(0,kcol+now(t)//nb)),
          pl.BlockSpec((full,128),lambda t:(0,vcol+was(t)//nb)),
          pl.BlockSpec((2,IB),lambda t:(0,now(t)%nb)),
          pl.BlockSpec((2,full,128),lambda t:(0,0,0)),
          pl.BlockSpec((1,2,8,128),lambda t:(now(t)//nb,0,0,0)),
          pl.BlockSpec((128,2*full),lambda t:(0,0))],
        out_specs=[pl.BlockSpec((IB,128),lambda t:(was(t)%nb,was(t)//nb)),
          pl.BlockSpec((2,1,full,IB),lambda t:(was(t)//nb,was(t)%nb,0,0)),
          pl.BlockSpec((1,8,IB),lambda t:(was(t)//nb,0,was(t)%nb))],
        out_shape=[jax.ShapeDtypeStruct((full,width),BF),
          jax.ShapeDtypeStruct((heads,nb,full,IB),BF),
          jax.ShapeDtypeStruct((pairs,8,full),F32)],
        scratch_shapes=[pltpu.VMEM((2,nb,full,IB),jnp.int32),pltpu.VMEM((128,2*full),jnp.int32),
          pltpu.VMEM((144,full),BF),pltpu.VMEM((full,256),BF),pltpu.VMEM((2,full,IB),F32),pltpu.VMEM((2,full,IB),F32),
          pltpu.VMEM((8,IB),F32)],
        compiler_params=pltpu.CompilerParams(vmem_limit_bytes=48*1024*1024),
        cost_estimate=pl.CostEstimate(flops=1000,bytes_accessed=1000,transcendentals=0),
        name="attend",
    )(length,q,k,v,crow,ccol,tab,nidx)

def bwd_kernel(q_ref,k_ref,v_ref,go_ref,ctx_ref,p_ref,linv_ref,
               g3_ref,ds_ref,diag_ref,
               kt_ref,acc_ref,wide_ref,gp_ref):
    g=pl.program_id(0); b=pl.program_id(1); nb=pl.num_programs(1)
    full=k_ref.shape[0]
    nj=full//JC
    @pl.when(b==0)
    def _():
        kt_ref[...]=k_ref[...].T
        acc_ref[...]=jnp.zeros_like(acc_ref)
        wide_ref[...]=jnp.zeros_like(wide_ref)
    gt=go_ref[...].astype(F32).T
    ct=ctx_ref[...].astype(F32).T
    rowi=lax.broadcasted_iota(jnp.int32,(128,IB),0)
    inv=jnp.where(rowi<64,jnp.broadcast_to(linv_ref[0,0:1,:],(128,IB)),jnp.broadcast_to(linv_ref[0,1:2,:],(128,IB)))
    gs=gt*inv
    pr=gs*ct
    gsb=gs.astype(BF)
    gos=gs.T.astype(BF)
    lane=lax.broadcasted_iota(jnp.int32,(IB,128),1)
    q2=q_ref[...]
    zero=jnp.zeros_like(q2)
    qs=[];gg=[];dqs=[];dds=[]
    for h in range(2):
        keep=(lane<64)==(h==0)
        qs.append(jnp.where(keep,q2,zero)); gg.append(jnp.where(keep,gos,zero))
        dd=jnp.sum(pr[64*h:64*h+64],axis=0,keepdims=True)
        gh=jnp.where((rowi<64)==(h==0),gsb,jnp.zeros_like(gsb))
        gp_ref[h]=nn(v_ref[...],gh)
        dds.append(dd)
    for h in range(2):
        for m in range(nj):
            rows=slice(m*JC,(m+1)*JC)
            ds=p_ref[h,0,rows,:].astype(F32)*(gp_ref[h,rows,:]-dds[h])
            ds_ref[h,0,rows,:]=ds.astype(BF)
            sl=pl.ds(pl.multiple_of(b*IB+(full-m*JC),128),IB)
            wide_ref[h,:,sl]=wide_ref[h,:,sl]+ds
        dqs.append(nn(kt_ref[64*h:64*h+64,:],ds_ref[h,0]))
    qcat=jnp.concatenate(qs,axis=0); gcat=jnp.concatenate(gg,axis=0)
    acc_ref[0]+=nn(jnp.concatenate([ds_ref[0,0],ds_ref[1,0]],axis=1),qcat)
    acc_ref[1]+=nn(jnp.concatenate([p_ref[0,0],p_ref[1,0]],axis=1),gcat)
    g3_ref[0,pl.ds(pl.multiple_of(b*IB,IB),IB),:]=(jnp.concatenate(dqs,axis=0)*0.125).T.astype(BF)
    @pl.when(b==nb-1)
    def _():
        g3_ref[1]=(acc_ref[0]*0.125).astype(BF)
        g3_ref[2]=acc_ref[1].astype(BF)
        for h in range(2):
            tot=jnp.zeros((8,2*full),F32)
            for r in range(16):
                x=wide_ref[h,r*8:(r+1)*8,:]
                tot=tot+pltpu.roll(x,2*full-r*8,1) if r else tot+x
            one=tot[0:1]
            for r in range(1,8):
                one=one+pltpu.roll(tot[r:r+1],2*full-r,1)
            diag_ref[0,h:h+1,:]=one

def bwd_attention(q,k,v,qcol,kcol,vcol,go,ctx,p,linv,heads=12):
    full=q.shape[0]; width=heads*64; pairs=heads//2; nb=full//IB
    return pl.pallas_call(
        bwd_kernel, grid=(pairs,nb),
        in_specs=[pl.BlockSpec((IB,128),lambda g,b:(b,qcol+g)),
          pl.BlockSpec((full,128),lambda g,b:(0,kcol+g)),
          pl.BlockSpec((full,128),lambda g,b:(0,vcol+g)),
          pl.BlockSpec((IB,128),lambda g,b:(b,g)),
          pl.BlockSpec((IB,128),lambda g,b:(b,g)),
          pl.BlockSpec((2,1,full,IB),lambda g,b:(g,b,0,0)),
          pl.BlockSpec((1,8,IB),lambda g,b:(g,0,b))],
        out_specs=[pl.BlockSpec((3,full,128),lambda g,b:(0,0,g)),
          pl.BlockSpec((2,1,full,IB),lambda g,b:(g,b,0,0)),
          pl.BlockSpec((1,8,2*full),lambda g,b:(g,0,0))],
        out_shape=[jax.ShapeDtypeStruct((3,full,width),BF),
          jax.ShapeDtypeStruct((heads,nb,full,IB),BF),
          jax.ShapeDtypeStruct((pairs,8,2*full),F32)],
        scratch_shapes=[pltpu.VMEM((128,full),BF),pltpu.VMEM((2,full,128),F32),pltpu.VMEM((2,128,2*full),F32),pltpu.VMEM((2,full,IB),F32)],
        compiler_params=pltpu.CompilerParams(vmem_limit_bytes=48*1024*1024),
        cost_estimate=pl.CostEstimate(flops=1000,bytes_accessed=1000,transcendentals=0),
        input_output_aliases={5:1}, name="attend_back",
    )(q,k,v,go,ctx,p,linv)

THRESH=[-8192]+[1-e for e in reversed(FAR_EDGES)]+list(FAR_EDGES)
def hist_kernel(ds_ref, crow_ref, ccol_ref, out_ref, acc_ref, *, heads, dt):
    t=pl.program_id(0)
    nb=ds_ref.shape[1]
    sub=ds_ref.shape[2]//16
    @pl.when(t==0)
    def _(): acc_ref[...]=jnp.zeros_like(acc_ref)
    one=jnp.ones((16,IB),BF); zero=jnp.zeros((16,IB),BF)
    for u in range(sub):
        for kb in range(nb):
            parts=[]
            for kind in range(2):
                row=jnp.broadcast_to(crow_ref[kind:kind+1,kb*IB:(kb+1)*IB],(16,IB)).astype(dt)
                col=jnp.concatenate([ccol_ref[kind,u*16:(u+1)*16,:]]*(IB//128),axis=1)
                for e in range(32):
                    th=THRESH[min(e,30)]
                    parts.append(jnp.where(row<=(col-th).astype(dt),one,zero))
            lhs=jnp.concatenate(parts,axis=0)
            rhs=ds_ref[:,kb,u*16:(u+1)*16,:].reshape(heads*16,IB)
            acc_ref[...]+=nt(lhs,rhs)
    @pl.when(t==pl.num_programs(0)-1)
    def _():
        r=lax.broadcasted_iota(jnp.int32,(1024,heads*16),0); c=lax.broadcasted_iota(jnp.int32,(1024,heads*16),1)
        a=jnp.where((r%16)==(c%16),acc_ref[...],0.0)
        a=jnp.sum(a.reshape(64,16,heads*16),axis=1)
        out_ref[...]=a
def hist(ds,crow,ccol,heads=12,jb=32,dt=jnp.int32,part=0,parts=1):
    nb,full=ds.shape[1:3]; steps=full//jb//parts; at=part*steps
    return pl.pallas_call(functools.partial(hist_kernel,heads=heads,dt=dt),grid=(steps,),
        in_specs=[pl.BlockSpec((heads,nb,jb,IB),lambda t:(0,0,t+at,0)),
          pl.BlockSpec((2,full),lambda t:(0,0)),
          pl.BlockSpec((2,jb,128),lambda t:(0,t+at,0))],
        out_specs=pl.BlockSpec((64,heads*16),lambda t:(0,0)),
        out_shape=jax.ShapeDtypeStruct((64,heads*16),F32),
        scratch_shapes=[pltpu.VMEM((1024,heads*16),F32)],
        compiler_params=pltpu.CompilerParams(vmem_limit_bytes=48*1024*1024),
        cost_estimate=pl.CostEstimate(flops=HISTF,bytes_accessed=1000,transcendentals=0),
        name="bucket_sums")(ds,crow,ccol)

def np_level(d,edges):
    a=np.abs(d); r=np.zeros(d.shape,np.int32)
    for e in edges: r+=(a>=e)
    return r+16*(d>0)
def lanes_of():
    lane=np.arange(128)
    e=(lane%32)//2; half=lane%2
    a=np.where(e==0,0,np.where(e==1,1,2**np.maximum(e-1,0)+half*2**np.maximum(e-2,0)))
    return np_level(np.where((lane//32)%2==1,a,-a),FAR_EDGES)
def tables(bias_tables):
    near=np.arange(128)%32; far=lanes_of()
    spot=np.arange(96)
    hot=np.stack([spot==near[:,None],spot==(np.where(np.arange(128)<64,32,64)+far)[:,None]])
    t=jnp.einsum('klb,bh->hkl',jnp.asarray(hot,BF),bias_tables.reshape(96,-1),preferred_element_type=F32)
    t=jnp.round((t+4.0)*UNIT).astype(jnp.int32)
    t=t[0::2]+(t[1::2]<<16)
    return jnp.broadcast_to(t[:,:,None,:],(t.shape[0],2,8,128))
def near_idx(full):
    r=lax.broadcasted_iota(jnp.int32,(128,2*full),0); u=lax.broadcasted_iota(jnp.int32,(128,2*full),1)
    return level(r+full-u,NEAR_EDGES)


from jax.sharding import PartitionSpec as P

BOXQ = 1000
BOTH = ("docs", "half")
TIE = -1


def fourier(coords):
    scaled = coords.astype(F32) / BOXQ
    freqs = (jnp.arange(16, dtype=F32) + 1.0) * math.pi
    angle = scaled[:, :, None] * freqs[None, None, :]
    waves = jnp.concatenate([jnp.sin(angle), jnp.cos(angle)], axis=2)
    return jnp.transpose(waves, (1, 0, 2)).reshape(coords.shape[1], 128)


def layer_norm(resid, gain, shift):
    centre = resid - jnp.mean(resid, axis=-1, keepdims=True)
    spread = jnp.mean(centre * centre, axis=-1, keepdims=True)
    return centre * lax.rsqrt(spread + 1e-06) * gain + shift


def gelu_pair(x):
    bell = jnp.exp2(x * x * (-0.5 * LOG2E))
    t = 1.0 / (1.0 + (0.3275911 * math.sqrt(0.5)) * jnp.abs(x))
    poly = t * (0.254829592 + t * (-0.284496736 + t * (1.421413741 + t * (-1.453152027 + t * 1.061405429))))
    tail = 0.5 * poly * bell
    cdf = jnp.where(x < 0, tail, 1.0 - tail)
    return x * cdf, cdf + x * bell * (1.0 / math.sqrt(2.0 * math.pi))


def inner(left, right):
    return lax.dot_general(left, right, (((0,), (0,)), ((), ())), preferred_element_type=F32)


def far_table(sums):
    total = sums[0]
    count = len(FAR_EDGES)
    below = [total - sums[count - i] for i in range(count)]
    above = [sums[count + 1 + i] for i in range(count)]
    zero = jnp.zeros_like(total)
    rows = [total - below[0] - above[0]]
    for side in (below, above):
        edges = side + [zero]
        rows += [edges[i] - edges[i + 1] for i in range(count)]
        if side is below:
            rows.append(zero)
    return jnp.stack(rows)


def swap(part, me):
    own = jnp.where(me == 0, part[0], part[1])
    other = jnp.where(me == 0, part[1], part[0])
    came = lax.ppermute(other, "half", [(0, 1), (1, 0)])
    return jnp.concatenate([jnp.where(me == 0, own, came), jnp.where(me == 0, came, own)], axis=0)


def unswap(whole, me):
    rows = whole.shape[0] // 2
    own = jnp.where(me == 0, whole[:rows], whole[rows:])
    other = jnp.where(me == 0, whole[rows:], whole[:rows])
    came = lax.ppermute(other, "half", [(0, 1), (1, 0)])
    return jnp.stack([jnp.where(me == 0, own, came), jnp.where(me == 0, came, own)])


class Route:
    def __init__(self):
        docs = lax.axis_size("docs")
        bits = [("docs", 1 << i) for i in range(docs.bit_length() - 1)]
        self.core = bits[0]
        y = ("half", 1)
        self.orders = [bits[1:2] + [y] + bits[2:], [y] + bits[1:], bits[2:] + bits[1:2] + [y]]
        self.all = bits + [y]
        self.pieces = docs * 2 // 2

    def mine(self, step):
        return (lax.axis_index(step[0]) // step[1]) % 2

    def move(self, x, step):
        axis, bit = step
        return lax.ppermute(x, axis, [(i, i ^ bit) for i in range(lax.axis_size(axis))])

    def product(self, left, right):
        mine = self.mine(self.core)
        cols = left.shape[1] // 2
        dot = lambda at: jnp.einsum("td,...tf->...df", lax.dynamic_slice_in_dim(left, at * cols, cols, 1), right,
                                    preferred_element_type=F32)
        send = dot(1 - mine).astype(BF)
        keep = dot(mine)
        return (keep + self.move(send, self.core).astype(F32)).astype(BF)

    def scatter(self, x, step):
        mine = self.mine(step)
        half = x.shape[0] // 2
        send = lax.dynamic_slice_in_dim(x, (1 - mine) * half, half, 0)
        keep = lax.dynamic_slice_in_dim(x, mine * half, half, 0)
        return (keep.astype(F32) + self.move(send, step).astype(F32)).astype(BF)

    def gather(self, x, step):
        mine = self.mine(step)
        came = self.move(x, step)
        return jnp.concatenate([jnp.where(mine == 0, x, came), jnp.where(mine == 0, came, x)], axis=0)

    def total(self, parts, between=None):
        rows = [p.shape[0] // self.pieces for p in parts]
        x = jnp.concatenate([p.reshape(self.pieces, r, p.shape[1]) for p, r in zip(parts, rows)], axis=1)
        count = x.shape[1]
        x = jnp.pad(x, ((0, 0), (0, -count % 16), (0, 0)))
        cut = x.shape[1] // 2
        lanes = [x[:, :cut], x[:, cut:]]
        hold = lambda i, lanes: between(i, lanes) if between and i < 7 else lanes
        lanes = hold(0, lanes)
        stages = len(self.orders[0])
        for i in range(stages):
            lanes = hold(1 + i, lanes)
            lanes = [self.scatter(x, order[i]) for x, order in zip(lanes, self.orders)]
        for i in reversed(range(stages)):
            lanes = hold(2 * stages - i, lanes) if stages == 4 else lanes
            lanes = [self.gather(x, order[i]) for x, order in zip(lanes, self.orders)]
        came = [self.move(x, self.core) for x in lanes]
        mine = self.mine(self.core)
        own, came = jnp.concatenate(lanes, axis=1), jnp.concatenate(came, axis=1)
        whole = jnp.concatenate([jnp.where(mine == 0, own, came), jnp.where(mine == 0, came, own)], axis=0)
        out = []
        at = 0
        for p, r in zip(parts, rows):
            out.append(whole[:, at:at + r].reshape(-1, p.shape[1]).astype(F32))
            at += r
        return out

    def small(self, parts):
        sizes = [p.size for p in parts]
        flat = jnp.concatenate([p.reshape(-1) for p in parts])
        count = flat.shape[0]
        flat = jnp.pad(flat, (0, -count % 1024)).reshape(-1, 128)
        for step in self.all:
            flat = flat + self.move(flat, step)
        flat = flat.reshape(-1)
        out = []
        at = 0
        for p, n in zip(parts, sizes):
            out.append(flat[at:at + n].reshape(p.shape))
            at += n
        return out


def shards(hidden_in, boxes, lengths, cotangent, layout_weight, qkv_weight, qv_bias, bias_tables, out_weight,
           out_bias, norm1_gain, norm1_bias, ff_in, ff_in_bias, ff_out, ff_out_bias, norm2_gain, norm2_bias):
    width = hidden_in.shape[2]
    full = boxes.shape[2]
    heads = bias_tables.shape[2]
    me = lax.axis_index("half")
    route = Route()
    hidden = swap(hidden_in, me)
    box = lax.dynamic_index_in_dim(boxes, me, 1, keepdims=False)
    length = lax.dynamic_slice_in_dim(lengths, me, 1, 0)
    feats = fourier(box).astype(BF)
    crow = jnp.stack([box[0] + box[2], box[1] + box[3]])
    ccol = jnp.broadcast_to(crow[:, :, None], (2, full, 128))
    packed = tables(bias_tables)
    skew = near_idx(full)
    bias3 = jnp.concatenate([qv_bias[0], jnp.zeros_like(qv_bias[0]), qv_bias[1]]).astype(F32)
    hidden, feats, ccol, packed, skew, bias3 = lax.optimization_barrier((hidden, feats, ccol, packed, skew, bias3))
    start = hidden.astype(F32) + nn(feats, layout_weight)
    start_low = start.astype(BF)
    qkv = (nn(start_low, qkv_weight) + bias3).astype(BF)
    pairs = heads // 2
    context, probs, linv = fwd_attention(
        qkv, qkv, qkv, 0, pairs, 2 * pairs, length, crow, ccol, packed, skew, heads)
    upstream = swap(cotangent, me).astype(F32)
    attended = nn(context, out_weight) + out_bias.astype(F32)
    mid, norm1_pull = jax.vjp(layer_norm, start + attended, norm1_gain.astype(F32), norm1_bias.astype(F32))
    mid_low = mid.astype(BF)
    hidden_pre = nn(mid_low, ff_in) + ff_in_bias.astype(F32)
    activated, slope = gelu_pair(hidden_pre)
    activated = activated.astype(BF)
    activated, slope = lax.optimization_barrier((activated, slope.astype(BF)))
    branch = nn(activated, ff_out) + ff_out_bias.astype(F32)
    result, norm2_pull = jax.vjp(layer_norm, mid + branch, norm2_gain.astype(F32), norm2_bias.astype(F32))
    layer_out = unswap(result.astype(BF), me)
    grad_r2, gain2_grad, shift2_grad = norm2_pull(upstream)
    grad_ff = grad_r2.astype(BF)
    ffout_part = inner(activated, grad_ff).astype(BF)
    ffoutb_grad = jnp.sum(grad_ff.astype(F32), axis=0)
    grad_inner = (nt(grad_ff, ff_out) * slope.astype(F32)).astype(BF)
    ffin_part = inner(mid_low, grad_inner).astype(BF)
    ffinb_grad = nn(jnp.ones((8, full), BF), grad_inner)[0]
    grad_mid = grad_r2 + nt(grad_inner, ff_in)
    grad_r1, gain1_grad, shift1_grad = norm1_pull(grad_mid)
    grad_att = grad_r1.astype(BF)
    outw_part = inner(context, grad_att).astype(BF)
    outb_grad = jnp.sum(grad_att.astype(F32), axis=0)
    grad_context = nt(grad_att, out_weight).astype(BF)
    early = (ffout_part, ffin_part, outw_part)
    grad_context = lax.optimization_barrier((*early, grad_context))[-1]
    early = lax.psum(early, BOTH)
    grad3, gscores, diag = bwd_attention(
        qkv, qkv, qkv, 0, pairs, 2 * pairs, grad_context, context, probs, linv, heads)
    qkv_part = route.product(start_low, grad3)
    qvb_grad = jnp.sum(grad3.astype(F32), axis=1)[0::2]
    grad_start = (grad_r1 + sum(nt(grad3[c], qkv_weight[:, c * width:(c + 1) * width]) for c in range(3))).astype(BF)
    input_grad = unswap(grad_start, me)
    lay_part = route.product(feats, grad_start)
    plan = [1, 2, 1, 1, 1, 1, 1]
    bucket_parts = []

    def between(i, lanes):
        row = crow
        if i:
            row, *lanes = lax.optimization_barrier((crow, *lanes))
        for _ in range(plan[i]):
            bucket_parts.append(hist(gscores, row, ccol, heads, dt=jnp.int16, part=len(bucket_parts), parts=sum(plan)))
        return lanes

    late = [qkv_part[0], qkv_part[1], qkv_part[2], lay_part]
    groups = route.total(late, between)
    assert len(bucket_parts) == sum(plan)
    sums = jnp.sum(sum(bucket_parts).reshape(2, 32, heads, 16), axis=3)
    offset = lax.broadcasted_iota(jnp.int32, (2 * full, 32), 0)
    bucket = lax.broadcasted_iota(jnp.int32, (2 * full, 32), 1)
    near_hot = (level(full - offset, NEAR_EDGES) == bucket).astype(F32)
    diag = diag[:, :2].reshape(heads, 2 * full)
    near_grad = lax.dot_general(near_hot, diag, (((0,), (1,)), ((), ())), precision=lax.Precision.HIGHEST)
    table_grad = jnp.stack([near_grad, far_table(sums[0]), far_table(sums[1])])

    qkv_total = jnp.concatenate(groups[:3], axis=1)
    lay_total = groups[3]
    (ffinb_total, ffoutb_total, gain2_total, shift2_total, outb_total, gain1_total, shift1_total, qvb_total,
     table_total) = route.small([ffinb_grad, ffoutb_grad, gain2_grad, shift2_grad, outb_grad, gain1_grad, shift1_grad,
                                 qvb_grad, table_grad])
    ffout_total, ffin_total, outw_total = (x.astype(F32) for x in early)
    return (layer_out, input_grad, lay_total, qkv_total, qvb_total, table_total, outw_total,
            outb_total, gain1_total, shift1_total, ffin_total, ffinb_total, ffout_total, ffoutb_total,
            gain2_total, shift2_total)


def solution(mesh):
    placed = (P("docs", "half", None), P(None, "docs", None), P("docs"), P("docs", "half", None)) + (P(),) * 14
    return jax.shard_map(
        shards, mesh=mesh, in_specs=placed,
        out_specs=(P("docs", "half", None), P("docs", "half", None)) + (P(),) * 14, check_vma=False)
```

```python
import functools, math
import numpy as np
import jax, jax.numpy as jnp
from jax import lax
from jax.experimental import pallas as pl
from jax.experimental.pallas import tpu as pltpu

BF=jnp.bfloat16; F32=jnp.float32
NEAR_EDGES = (1, 2, 3, 4, 5, 6, 7, 8, 12, 16, 24, 32, 64, 128, 256)
FAR_EDGES = (1, 2, 4, 8, 16, 32, 64, 96, 128, 192, 256, 384, 512, 768, 1024)
LOG2E=math.log2(math.e)
HISTF=15*10**9
IB=256
FC=256
JC=128

def nt(a,b):
    return lax.dot_general(a,b,(((1,),(1,)),((),())),preferred_element_type=F32)
def nn(a,b):
    return lax.dot_general(a,b,(((1,),(0,)),((),())),preferred_element_type=F32)
def level(rel, edges):
    magnitude = jnp.abs(rel)
    result = jnp.zeros(rel.shape, jnp.int32)
    for edge in edges:
        result = result + (magnitude >= edge).astype(jnp.int32)
    return result + 16 * (rel > 0).astype(jnp.int32)

def lookup(table, idx):
    rows=idx.shape[0]
    t=jnp.broadcast_to(table[0:1], (rows,128))
    return jnp.take_along_axis(t, idx, axis=1, mode="promise_in_bounds")

UNIT=2048.0

def far_lane(d):
    a=jnp.abs(d)
    e=32-lax.clz(a)
    half=lax.shift_right_logical(a,jnp.maximum(e-2,0))&1
    return 2*e+half+jnp.where(d>0,32,0)

def fwd_kernel(len_ref, q_ref, k_ref, v_ref, cq_ref, ck_ref, tab_ref, nidx_ref,
               ctx_ref, p_ref, linv_ref, idx_ref, wide_ref, vt_ref, ka_ref, s0_ref, s1_ref, top_ref):
    t=pl.program_id(0)
    full=k_ref.shape[0]
    nj=full//JC; nb=full//IB
    last=pl.num_programs(0)-2
    now=jnp.minimum(t,last); before=jnp.maximum(t-1,0)
    g=now//nb; b=now%nb
    @pl.when(t<nb)
    def _():
        for m in range(nj):
            rows=slice(m*JC,(m+1)*JC)
            for c in range(IB//128):
                for kind in range(2):
                    idx_ref[kind,b,rows,c*128:(c+1)*128]=far_lane(ck_ref[kind,rows,:]-cq_ref[kind:kind+1,c*128:(c+1)*128])+64*kind
    @pl.when(t==0)
    def _():
        key=lax.broadcasted_iota(jnp.int32,(full,128),0); lane=lax.broadcasted_iota(jnp.int32,(full,128),1)
        ka_ref[:,128:]=jnp.where((key>=len_ref[0])&(lane==0),-1e30,0.0).astype(BF)
        vt_ref[128:144,:]=jnp.ones((16,full),BF)
        s1_ref[...]=jnp.zeros_like(s1_ref)
        top_ref[...]=jnp.zeros_like(top_ref)
    @pl.when(b==0)
    def _():
        ka_ref[:,:128]=k_ref[...]
        first,count=near_span(full)
        table=tab_ref[0,0]
        wide_ref[:,:first*128]=jnp.broadcast_to(table[0:1,31:32],(128,first*128))
        for c in range(count):
            wide_ref[:,(first+c)*128:(first+c+1)*128]=lookup(table,nidx_ref[:,c*128:(c+1)*128])
        rest=2*full-(first+count)*128
        wide_ref[:,2*full-rest:]=jnp.broadcast_to(table[0:1,15:16],(128,rest))
    @pl.when(before%nb==0)
    def _():
        vt_ref[0:128,:]=v_ref[...].T
    scale=LOG2E/UNIT
    def body(cur_ref,prev_ref):
        rowi=lax.broadcasted_iota(jnp.int32,(128,IB),0)
        qt=(q_ref[...]*jnp.asarray(0.125*UNIT,BF)).T
        qh=[jnp.concatenate([jnp.where((rowi<64)==(h==0),qt,jnp.zeros_like(qt)),jnp.ones_like(qt)],axis=0) for h in range(2)]
        mx=[top_ref[h:h+1,:]*scale for h in range(2)]
        top=[jnp.full((8,IB),-jnp.inf,F32)]*2
        lhs=[jnp.concatenate([vt_ref[64*h:64*h+64,:],vt_ref[128:144,:]],axis=0) for h in range(2)]
        acc=[jnp.zeros((80,IB),F32)]*2
        for m in range(full//FC):
            rows=slice(m*FC,(m+1)*FC)
            raw=[nn(ka_ref[rows,:],qh[h]) for h in range(2)]
            for h in range(2):
                p=jnp.exp2(prev_ref[h,rows,:]*scale-mx[h]).astype(BF)
                p_ref[h,0,rows,:]=p
                acc[h]=acc[h]+nn(lhs[h][:,rows],p)
            near=jnp.concatenate([wide_ref[:,pl.ds(pl.multiple_of(b*IB+(full-w*JC),128),IB)] for w in range(m*FC//JC,(m+1)*FC//JC)],axis=0)
            x=near+jnp.concatenate([lookup(tab_ref[0,1],idx_ref[0,b,rows,c*128:(c+1)*128])+lookup(tab_ref[0,1],idx_ref[1,b,rows,c*128:(c+1)*128]) for c in range(IB//128)],axis=1)
            for h in range(2):
                y=(x&0xffff) if h==0 else lax.shift_right_logical(x,16)
                s=raw[h]+y.astype(F32)
                cur_ref[h,rows,:]=s
                top[h]=jnp.maximum(top[h],jnp.max(s.reshape(FC//8,8,IB),axis=0))
        outs=[]
        for h in range(2):
            top_ref[h:h+1,:]=jnp.max(top[h],axis=0,keepdims=True)
            inv=1.0/acc[h][64:65]
            linv_ref[0,h:h+1,:]=inv
            outs.append(acc[h][:64]*inv)
        ctx_ref[...]=jnp.concatenate(outs,axis=0).T.astype(BF)
    @pl.when(t%2==0)
    def _(): body(s0_ref,s1_ref)
    @pl.when(t%2==1)
    def _(): body(s1_ref,s0_ref)

def fwd_attention(q,k,v,qcol,kcol,vcol,length,crow,ccol,tab,nidx,heads=12):
    full=q.shape[0]; width=heads*64; pairs=heads//2; nb=full//IB; last=pairs*nb-1
    now=lambda t: jnp.minimum(t,last)
    was=lambda t: jnp.maximum(t-1,0)
    return pl.pallas_call(
        fwd_kernel, grid=(pairs*nb+1,),
        in_specs=[pl.BlockSpec(memory_space=pltpu.SMEM),
          pl.BlockSpec((IB,128),lambda t:(now(t)%nb,qcol+now(t)//nb)),
          pl.BlockSpec((full,128),lambda t:(0,kcol+now(t)//nb)),
          pl.BlockSpec((full,128),lambda t:(0,vcol+was(t)//nb)),
          pl.BlockSpec((2,IB),lambda t:(0,now(t)%nb)),
          pl.BlockSpec((2,full,128),lambda t:(0,0,0)),
          pl.BlockSpec((1,2,8,128),lambda t:(now(t)//nb,0,0,0)),
          pl.BlockSpec((128,nidx.shape[1]),lambda t:(0,0))],
        out_specs=[pl.BlockSpec((IB,128),lambda t:(was(t)%nb,was(t)//nb)),
          pl.BlockSpec((2,1,full,IB),lambda t:(was(t)//nb,was(t)%nb,0,0)),
          pl.BlockSpec((1,8,IB),lambda t:(was(t)//nb,0,was(t)%nb))],
        out_shape=[jax.ShapeDtypeStruct((full,width),BF),
          jax.ShapeDtypeStruct((heads,nb,full,IB),BF),
          jax.ShapeDtypeStruct((pairs,8,full),F32)],
        scratch_shapes=[pltpu.VMEM((2,nb,full,IB),jnp.int32),pltpu.VMEM((128,2*full),jnp.int32),
          pltpu.VMEM((144,full),BF),pltpu.VMEM((full,256),BF),pltpu.VMEM((2,full,IB),F32),pltpu.VMEM((2,full,IB),F32),
          pltpu.VMEM((8,IB),F32)],
        compiler_params=pltpu.CompilerParams(vmem_limit_bytes=48*1024*1024),
        cost_estimate=pl.CostEstimate(flops=1000,bytes_accessed=1000,transcendentals=0),
        name="attend",
    )(length,q,k,v,crow,ccol,tab,nidx)

def bwd_kernel(q_ref,k_ref,v_ref,go_ref,ctx_ref,p_ref,linv_ref,
               g3_ref,ds_ref,diag_ref,
               kt_ref,acc_ref,wide_ref,gp_ref):
    g=pl.program_id(0); b=pl.program_id(1); nb=pl.num_programs(1)
    full=k_ref.shape[0]
    nj=full//JC
    @pl.when(b==0)
    def _():
        kt_ref[...]=k_ref[...].T
        acc_ref[...]=jnp.zeros_like(acc_ref)
        wide_ref[...]=jnp.zeros_like(wide_ref)
    gt=go_ref[...].astype(F32).T
    ct=ctx_ref[...].astype(F32).T
    rowi=lax.broadcasted_iota(jnp.int32,(128,IB),0)
    inv=jnp.where(rowi<64,jnp.broadcast_to(linv_ref[0,0:1,:],(128,IB)),jnp.broadcast_to(linv_ref[0,1:2,:],(128,IB)))
    gs=gt*inv
    pr=gs*ct
    gsb=gs.astype(BF)
    gos=gs.T.astype(BF)
    lane=lax.broadcasted_iota(jnp.int32,(IB,128),1)
    q2=q_ref[...]
    zero=jnp.zeros_like(q2)
    qs=[];gg=[];dqs=[];dds=[]
    for h in range(2):
        keep=(lane<64)==(h==0)
        qs.append(jnp.where(keep,q2,zero)); gg.append(jnp.where(keep,gos,zero))
        dd=jnp.sum(pr[64*h:64*h+64],axis=0,keepdims=True)
        gh=jnp.where((rowi<64)==(h==0),gsb,jnp.zeros_like(gsb))
        gp_ref[h]=nn(v_ref[...],gh)
        dds.append(dd)
    for h in range(2):
        for m in range(nj):
            rows=slice(m*JC,(m+1)*JC)
            ds=p_ref[h,0,rows,:].astype(F32)*(gp_ref[h,rows,:]-dds[h])
            ds_ref[h,0,rows,:]=ds.astype(BF)
            sl=pl.ds(pl.multiple_of(b*IB+(full-m*JC),128),IB)
            wide_ref[h,:,sl]=wide_ref[h,:,sl]+ds
        dqs.append(nn(kt_ref[64*h:64*h+64,:],ds_ref[h,0]))
    qcat=jnp.concatenate(qs,axis=0); gcat=jnp.concatenate(gg,axis=0)
    acc_ref[0]+=nn(jnp.concatenate([ds_ref[0,0],ds_ref[1,0]],axis=1),qcat)
    acc_ref[1]+=nn(jnp.concatenate([p_ref[0,0],p_ref[1,0]],axis=1),gcat)
    g3_ref[0,pl.ds(pl.multiple_of(b*IB,IB),IB),:]=(jnp.concatenate(dqs,axis=0)*0.125).T.astype(BF)
    @pl.when(b==nb-1)
    def _():
        g3_ref[1]=(acc_ref[0]*0.125).astype(BF)
        g3_ref[2]=acc_ref[1].astype(BF)
        for h in range(2):
            tot=jnp.zeros((8,2*full),F32)
            for r in range(16):
                x=wide_ref[h,r*8:(r+1)*8,:]
                tot=tot+pltpu.roll(x,2*full-r*8,1) if r else tot+x
            one=tot[0:1]
            for r in range(1,8):
                one=one+pltpu.roll(tot[r:r+1],2*full-r,1)
            diag_ref[0,h:h+1,:]=one

def bwd_attention(q,k,v,qcol,kcol,vcol,go,ctx,p,linv,heads=12):
    full=q.shape[0]; width=heads*64; pairs=heads//2; nb=full//IB
    return pl.pallas_call(
        bwd_kernel, grid=(pairs,nb),
        in_specs=[pl.BlockSpec((IB,128),lambda g,b:(b,qcol+g)),
          pl.BlockSpec((full,128),lambda g,b:(0,kcol+g)),
          pl.BlockSpec((full,128),lambda g,b:(0,vcol+g)),
          pl.BlockSpec((IB,128),lambda g,b:(b,g)),
          pl.BlockSpec((IB,128),lambda g,b:(b,g)),
          pl.BlockSpec((2,1,full,IB),lambda g,b:(g,b,0,0)),
          pl.BlockSpec((1,8,IB),lambda g,b:(g,0,b))],
        out_specs=[pl.BlockSpec((3,full,128),lambda g,b:(0,0,g)),
          pl.BlockSpec((2,1,full,IB),lambda g,b:(g,b,0,0)),
          pl.BlockSpec((1,8,2*full),lambda g,b:(g,0,0))],
        out_shape=[jax.ShapeDtypeStruct((3,full,width),BF),
          jax.ShapeDtypeStruct((heads,nb,full,IB),BF),
          jax.ShapeDtypeStruct((pairs,8,2*full),F32)],
        scratch_shapes=[pltpu.VMEM((128,full),BF),pltpu.VMEM((2,full,128),F32),pltpu.VMEM((2,128,2*full),F32),pltpu.VMEM((2,full,IB),F32)],
        compiler_params=pltpu.CompilerParams(vmem_limit_bytes=48*1024*1024),
        cost_estimate=pl.CostEstimate(flops=1000,bytes_accessed=1000,transcendentals=0),
        input_output_aliases={5:1}, name="attend_back",
    )(q,k,v,go,ctx,p,linv)

THRESH=[-8192]+[1-e for e in reversed(FAR_EDGES)]+list(FAR_EDGES)
def hist_kernel(ds_ref, crow_ref, ccol_ref, out_ref, acc_ref, lhs_ref, *, heads, dt):
    t=pl.program_id(0)
    nb=ds_ref.shape[1]
    sub=ds_ref.shape[2]//16
    @pl.when(t==0)
    def _(): acc_ref[...]=jnp.zeros_like(acc_ref)
    one=jnp.ones((16,IB),BF); zero=jnp.zeros((16,IB),BF)
    for u in range(sub):
        total=None
        for kb in range(nb):
            parts=[]
            for kind in range(2):
                row=jnp.broadcast_to(crow_ref[kind:kind+1,kb*IB:(kb+1)*IB],(16,IB)).astype(dt)
                col=jnp.concatenate([ccol_ref[kind,u*16:(u+1)*16,:]]*(IB//128),axis=1)
                less=row-col.astype(dt)
                for e in range(32):
                    parts.append(jnp.where(less<=jnp.asarray(-THRESH[min(e,30)],dt),one,zero))
            lhs_ref[u%2,:,kb*IB:(kb+1)*IB]=jnp.concatenate(parts,axis=0)
        rhs=jnp.concatenate([ds_ref[:,kb,u*16:(u+1)*16,:].reshape(heads*16,IB) for kb in range(nb)],axis=1)
        acc_ref[...]+=nt(lhs_ref[u%2],rhs)
    @pl.when(t==pl.num_programs(0)-1)
    def _():
        r=lax.broadcasted_iota(jnp.int32,(1024,heads*16),0); c=lax.broadcasted_iota(jnp.int32,(1024,heads*16),1)
        a=jnp.where((r%16)==(c%16),acc_ref[...],0.0)
        a=jnp.sum(a.reshape(64,16,heads*16),axis=1)
        out_ref[...]=a
def hist(ds,crow,ccol,heads=12,jb=32,dt=jnp.int32,part=0,parts=1):
    nb,full=ds.shape[1:3]; steps=full//jb//parts; at=part*steps
    return pl.pallas_call(functools.partial(hist_kernel,heads=heads,dt=dt),grid=(steps,),
        in_specs=[pl.BlockSpec((heads,nb,jb,IB),lambda t:(0,0,t+at,0)),
          pl.BlockSpec((2,full),lambda t:(0,0)),
          pl.BlockSpec((2,jb,128),lambda t:(0,t+at,0))],
        out_specs=pl.BlockSpec((64,heads*16),lambda t:(0,0)),
        out_shape=jax.ShapeDtypeStruct((64,heads*16),F32),
        scratch_shapes=[pltpu.VMEM((1024,heads*16),F32),pltpu.VMEM((2,1024,full),BF)],
        compiler_params=pltpu.CompilerParams(vmem_limit_bytes=48*1024*1024),
        cost_estimate=pl.CostEstimate(flops=HISTF,bytes_accessed=1000,transcendentals=0),
        name="bucket_sums")(ds,crow,ccol)

def np_level(d,edges):
    a=np.abs(d); r=np.zeros(d.shape,np.int32)
    for e in edges: r+=(a>=e)
    return r+16*(d>0)
def lanes_of():
    lane=np.arange(128)
    e=(lane%32)//2; half=lane%2
    a=np.where(e==0,0,np.where(e==1,1,2**np.maximum(e-1,0)+half*2**np.maximum(e-2,0)))
    return np_level(np.where((lane//32)%2==1,a,-a),FAR_EDGES)
def tables(bias_tables):
    near=np.arange(128)%32; far=lanes_of()
    spot=np.arange(96)
    hot=np.stack([spot==near[:,None],spot==(np.where(np.arange(128)<64,32,64)+far)[:,None]])
    t=jnp.einsum('klb,bh->hkl',jnp.asarray(hot,BF),bias_tables.reshape(96,-1),preferred_element_type=F32)
    t=jnp.round((t+4.0)*UNIT).astype(jnp.int32)
    t=t[0::2]+(t[1::2]<<16)
    return jnp.broadcast_to(t[:,:,None,:],(t.shape[0],2,8,128))
def near_span(full):
    kept=[c for c in range(2*full//128) if full-128*c-127<NEAR_EDGES[-1] and full-128*c+127>-NEAR_EDGES[-1]]
    return kept[0],len(kept)
def near_idx(full):
    first,count=near_span(full)
    r=lax.broadcasted_iota(jnp.int32,(128,count*128),0); u=first*128+lax.broadcasted_iota(jnp.int32,(128,count*128),1)
    return level(r+full-u,NEAR_EDGES)


from jax.sharding import PartitionSpec as P

BOXQ = 1000
BOTH = ("docs", "half")
TIE = -1


def fourier(coords):
    scaled = coords.astype(F32) / BOXQ
    freqs = (jnp.arange(16, dtype=F32) + 1.0) * math.pi
    angle = scaled[:, :, None] * freqs[None, None, :]
    waves = jnp.concatenate([jnp.sin(angle), jnp.cos(angle)], axis=2)
    return jnp.transpose(waves, (1, 0, 2)).reshape(coords.shape[1], 128)


def layer_norm(resid, gain, shift):
    centre = resid - jnp.mean(resid, axis=-1, keepdims=True)
    spread = jnp.mean(centre * centre, axis=-1, keepdims=True)
    return centre * lax.rsqrt(spread + 1e-06) * gain + shift


def gelu_pair(x):
    bell = jnp.exp2(x * x * (-0.5 * LOG2E))
    t = 1.0 / (1.0 + (0.3275911 * math.sqrt(0.5)) * jnp.abs(x))
    poly = t * (0.254829592 + t * (-0.284496736 + t * (1.421413741 + t * (-1.453152027 + t * 1.061405429))))
    tail = 0.5 * poly * bell
    cdf = jnp.where(x < 0, tail, 1.0 - tail)
    return x * cdf, cdf + x * bell * (1.0 / math.sqrt(2.0 * math.pi))


def inner(left, right):
    return lax.dot_general(left, right, (((0,), (0,)), ((), ())), preferred_element_type=F32)


def far_table(sums):
    total = sums[0]
    count = len(FAR_EDGES)
    below = [total - sums[count - i] for i in range(count)]
    above = [sums[count + 1 + i] for i in range(count)]
    zero = jnp.zeros_like(total)
    rows = [total - below[0] - above[0]]
    for side in (below, above):
        edges = side + [zero]
        rows += [edges[i] - edges[i + 1] for i in range(count)]
        if side is below:
            rows.append(zero)
    return jnp.stack(rows)


def swap(part, me):
    own = jnp.where(me == 0, part[0], part[1])
    other = jnp.where(me == 0, part[1], part[0])
    came = lax.ppermute(other, "half", [(0, 1), (1, 0)])
    return jnp.concatenate([jnp.where(me == 0, own, came), jnp.where(me == 0, came, own)], axis=0)


def unswap(whole, me):
    rows = whole.shape[0] // 2
    own = jnp.where(me == 0, whole[:rows], whole[rows:])
    other = jnp.where(me == 0, whole[rows:], whole[:rows])
    came = lax.ppermute(other, "half", [(0, 1), (1, 0)])
    return jnp.stack([jnp.where(me == 0, own, came), jnp.where(me == 0, came, own)])


class Route:
    def __init__(self):
        docs = lax.axis_size("docs")
        bits = [("docs", 1 << i) for i in range(docs.bit_length() - 1)]
        self.core = bits[0]
        y = ("half", 1)
        self.orders = [bits[1:2] + [y] + bits[2:], [y] + bits[1:], bits[2:] + bits[1:2] + [y]]
        self.all = bits + [y]
        self.pieces = docs * 2 // 2

    def mine(self, step):
        return (lax.axis_index(step[0]) // step[1]) % 2

    def move(self, x, step):
        axis, bit = step
        return lax.ppermute(x, axis, [(i, i ^ bit) for i in range(lax.axis_size(axis))])

    def product(self, left, right):
        mine = self.mine(self.core)
        cols = left.shape[1] // 2
        dot = lambda at: jnp.einsum("td,...tf->...df", lax.dynamic_slice_in_dim(left, at * cols, cols, 1), right,
                                    preferred_element_type=F32)
        send = dot(1 - mine).astype(BF)
        keep = dot(mine)
        return (keep + self.move(send, self.core).astype(F32)).astype(BF)

    def scatter(self, x, step):
        mine = self.mine(step)
        half = x.shape[0] // 2
        send = lax.dynamic_slice_in_dim(x, (1 - mine) * half, half, 0)
        keep = lax.dynamic_slice_in_dim(x, mine * half, half, 0)
        return (keep.astype(F32) + self.move(send, step).astype(F32)).astype(BF)

    def gather(self, x, step):
        mine = self.mine(step)
        came = self.move(x, step)
        return jnp.concatenate([jnp.where(mine == 0, x, came), jnp.where(mine == 0, came, x)], axis=0)

    def total(self, parts, between=None, last=None):
        rows = [p.shape[0] // self.pieces for p in parts]
        x = jnp.concatenate([p.reshape(self.pieces, r, p.shape[1]) for p, r in zip(parts, rows)], axis=1)
        count = x.shape[1]
        x = jnp.pad(x, ((0, 0), (0, -count % 16), (0, 0)))
        cut = x.shape[1] // 2
        lanes = [x[:, :cut], x[:, cut:]]
        hold = lambda i, lanes: between(i, lanes) if between and i < 7 else lanes
        lanes = hold(0, lanes)
        stages = len(self.orders[0])
        for i in range(stages):
            lanes = hold(1 + i, lanes)
            lanes = [self.scatter(x, order[i]) for x, order in zip(lanes, self.orders)]
        for i in reversed(range(stages)):
            lanes = hold(2 * stages - i, lanes) if stages == 4 else lanes
            lanes = [self.gather(x, order[i]) for x, order in zip(lanes, self.orders)]
        lanes = last(lanes) if last else lanes
        came = [self.move(x, self.core) for x in lanes]
        mine = self.mine(self.core)
        own, came = jnp.concatenate(lanes, axis=1), jnp.concatenate(came, axis=1)
        whole = jnp.concatenate([jnp.where(mine == 0, own, came), jnp.where(mine == 0, came, own)], axis=0)
        out = []
        at = 0
        for p, r in zip(parts, rows):
            out.append(whole[:, at:at + r].reshape(-1, p.shape[1]).astype(F32))
            at += r
        return out

    def small(self, parts):
        sizes = [p.size for p in parts]
        flat = jnp.concatenate([p.reshape(-1) for p in parts])
        count = flat.shape[0]
        flat = jnp.pad(flat, (0, -count % 1024)).reshape(-1, 128)
        for step in self.all:
            flat = flat + self.move(flat, step)
        flat = flat.reshape(-1)
        out = []
        at = 0
        for p, n in zip(parts, sizes):
            out.append(flat[at:at + n].reshape(p.shape))
            at += n
        return out


def shards(hidden_in, boxes, lengths, cotangent, layout_weight, qkv_weight, qv_bias, bias_tables, out_weight,
           out_bias, norm1_gain, norm1_bias, ff_in, ff_in_bias, ff_out, ff_out_bias, norm2_gain, norm2_bias):
    width = hidden_in.shape[2]
    full = boxes.shape[2]
    heads = bias_tables.shape[2]
    me = lax.axis_index("half")
    route = Route()
    hidden = swap(hidden_in, me)
    box = lax.dynamic_index_in_dim(boxes, me, 1, keepdims=False)
    length = lax.dynamic_slice_in_dim(lengths, me, 1, 0)
    feats = fourier(box).astype(BF)
    crow = jnp.stack([box[0] + box[2], box[1] + box[3]])
    ccol = jnp.broadcast_to(crow[:, :, None], (2, full, 128))
    packed = tables(bias_tables)
    skew = near_idx(full)
    bias3 = jnp.concatenate([qv_bias[0], jnp.zeros_like(qv_bias[0]), qv_bias[1]]).astype(F32)
    hidden, feats, ccol, packed, skew, bias3 = lax.optimization_barrier((hidden, feats, ccol, packed, skew, bias3))
    start = hidden.astype(F32) + nn(feats, layout_weight)
    start_low = start.astype(BF)
    qkv = (nn(start_low, qkv_weight) + bias3).astype(BF)
    pairs = heads // 2
    context, probs, linv = fwd_attention(
        qkv, qkv, qkv, 0, pairs, 2 * pairs, length, crow, ccol, packed, skew, heads)
    upstream = swap(cotangent, me).astype(F32)
    attended = nn(context, out_weight) + out_bias.astype(F32)
    mid, norm1_pull = jax.vjp(layer_norm, start + attended, norm1_gain.astype(F32), norm1_bias.astype(F32))
    mid_low = mid.astype(BF)
    hidden_pre = nn(mid_low, ff_in) + ff_in_bias.astype(F32)
    activated, slope = gelu_pair(hidden_pre)
    activated = activated.astype(BF)
    activated, slope = lax.optimization_barrier((activated, slope.astype(BF)))
    branch = nn(activated, ff_out) + ff_out_bias.astype(F32)
    result, norm2_pull = jax.vjp(layer_norm, mid + branch, norm2_gain.astype(F32), norm2_bias.astype(F32))
    layer_out = unswap(result.astype(BF), me)
    grad_r2, gain2_grad, shift2_grad = norm2_pull(upstream)
    grad_ff = grad_r2.astype(BF)
    ffout_part = inner(activated, grad_ff).astype(BF)
    ffoutb_grad = jnp.sum(grad_ff.astype(F32), axis=0)
    grad_inner = (nt(grad_ff, ff_out) * slope.astype(F32)).astype(BF)
    ffin_part = inner(mid_low, grad_inner).astype(BF)
    ffinb_grad = nn(jnp.ones((8, full), BF), grad_inner)[0]
    grad_mid = grad_r2 + nt(grad_inner, ff_in)
    grad_r1, gain1_grad, shift1_grad = norm1_pull(grad_mid)
    grad_att = grad_r1.astype(BF)
    outw_part = inner(context, grad_att).astype(BF)
    outb_grad = jnp.sum(grad_att.astype(F32), axis=0)
    grad_context = nt(grad_att, out_weight).astype(BF)
    early = (ffout_part, ffin_part, outw_part)
    grad_context = lax.optimization_barrier((*early, grad_context))[-1]
    early = lax.psum(early, BOTH)
    grad3, gscores, diag = bwd_attention(
        qkv, qkv, qkv, 0, pairs, 2 * pairs, grad_context, context, probs, linv, heads)
    qkv_part = route.product(start_low, grad3)
    qvb_grad = jnp.sum(grad3.astype(F32), axis=1)[0::2]
    grad_start = (grad_r1 + sum(nt(grad3[c], qkv_weight[:, c * width:(c + 1) * width]) for c in range(3))).astype(BF)
    input_grad = unswap(grad_start, me)
    lay_part = route.product(feats, grad_start)
    plan = [1, 2, 1, 1, 1, 1, 1]
    bucket_parts = []

    def between(i, lanes):
        row = crow
        if i:
            row, *lanes = lax.optimization_barrier((crow, *lanes))
        for _ in range(plan[i]):
            bucket_parts.append(hist(gscores, row, ccol, heads, dt=jnp.int16, part=len(bucket_parts), parts=sum(plan)))
        return lanes

    late = [qkv_part[0], qkv_part[1], qkv_part[2], lay_part]
    def last(lanes):
        nonlocal early
        *early, a, b = lax.optimization_barrier((*early, *lanes))
        return [a, b]

    groups = route.total(late, between, last)
    assert len(bucket_parts) == sum(plan)
    sums = jnp.sum(sum(bucket_parts).reshape(2, 32, heads, 16), axis=3)
    offset = lax.broadcasted_iota(jnp.int32, (2 * full, 32), 0)
    bucket = lax.broadcasted_iota(jnp.int32, (2 * full, 32), 1)
    near_hot = (level(full - offset, NEAR_EDGES) == bucket).astype(F32)
    diag = diag[:, :2].reshape(heads, 2 * full)
    near_grad = lax.dot_general(near_hot, diag, (((0,), (1,)), ((), ())), precision=lax.Precision.HIGHEST)
    table_grad = jnp.stack([near_grad, far_table(sums[0]), far_table(sums[1])])

    qkv_total = jnp.concatenate(groups[:3], axis=1)
    lay_total = groups[3]
    (ffinb_total, ffoutb_total, gain2_total, shift2_total, outb_total, gain1_total, shift1_total, qvb_total,
     table_total) = route.small([ffinb_grad, ffoutb_grad, gain2_grad, shift2_grad, outb_grad, gain1_grad, shift1_grad,
                                 qvb_grad, table_grad])
    ffout_total, ffin_total, outw_total = (x.astype(F32) for x in early)
    return (layer_out, input_grad, lay_total, qkv_total, qvb_total, table_total, outw_total,
            outb_total, gain1_total, shift1_total, ffin_total, ffinb_total, ffout_total, ffoutb_total,
            gain2_total, shift2_total)


def solution(mesh):
    placed = (P("docs", "half", None), P(None, "docs", None), P("docs"), P("docs", "half", None)) + (P(),) * 14
    return jax.shard_map(
        shards, mesh=mesh, in_specs=placed,
        out_specs=(P("docs", "half", None), P("docs", "half", None)) + (P(),) * 14, check_vma=False)
```

```python
import functools, math
import numpy as np
import jax, jax.numpy as jnp
from jax import lax
from jax.experimental import pallas as pl
from jax.experimental.pallas import tpu as pltpu

BF=jnp.bfloat16; F32=jnp.float32
NEAR_EDGES = (1, 2, 3, 4, 5, 6, 7, 8, 12, 16, 24, 32, 64, 128, 256)
FAR_EDGES = (1, 2, 4, 8, 16, 32, 64, 96, 128, 192, 256, 384, 512, 768, 1024)
LOG2E=math.log2(math.e)
HISTF=15*10**9
IB=256
FC=256
JC=128

def nt(a,b):
    return lax.dot_general(a,b,(((1,),(1,)),((),())),preferred_element_type=F32)
def nn(a,b):
    return lax.dot_general(a,b,(((1,),(0,)),((),())),preferred_element_type=F32)
def level(rel, edges):
    magnitude = jnp.abs(rel)
    result = jnp.zeros(rel.shape, jnp.int32)
    for edge in edges:
        result = result + (magnitude >= edge).astype(jnp.int32)
    return result + 16 * (rel > 0).astype(jnp.int32)

def lookup(table, idx):
    rows=idx.shape[0]
    t=jnp.broadcast_to(table[0:1], (rows,128))
    return jnp.take_along_axis(t, idx, axis=1, mode="promise_in_bounds")

UNIT=2048.0

def far_lane(d):
    a=jnp.abs(d)
    e=32-lax.clz(a)
    half=lax.shift_right_logical(a,jnp.maximum(e-2,0))&1
    return 2*e+half+jnp.where(d>0,32,0)

def fwd_kernel(len_ref, q_ref, k_ref, v_ref, cq_ref, ck_ref, tab_ref, nidx_ref,
               ctx_ref, p_ref, linv_ref, idx_ref, wide_ref, vt_ref, ka_ref, s0_ref, s1_ref, top_ref):
    t=pl.program_id(0)
    full=k_ref.shape[0]
    nj=full//JC; nb=full//IB
    last=pl.num_programs(0)-2
    now=jnp.minimum(t,last); before=jnp.maximum(t-1,0)
    g=now//nb; b=now%nb
    @pl.when(t<nb)
    def _():
        for m in range(nj):
            rows=slice(m*JC,(m+1)*JC)
            for c in range(IB//128):
                for kind in range(2):
                    idx_ref[kind,b,rows,c*128:(c+1)*128]=far_lane(ck_ref[kind,rows,:]-cq_ref[kind:kind+1,c*128:(c+1)*128])+64*kind
    @pl.when(t==0)
    def _():
        key=lax.broadcasted_iota(jnp.int32,(full,128),0); lane=lax.broadcasted_iota(jnp.int32,(full,128),1)
        ka_ref[:,128:]=jnp.where((key>=len_ref[0])&(lane==0),-1e30,0.0).astype(BF)
        vt_ref[128:144,:]=jnp.ones((16,full),BF)
        s1_ref[...]=jnp.zeros_like(s1_ref)
        top_ref[...]=jnp.zeros_like(top_ref)
    @pl.when(b==0)
    def _():
        ka_ref[:,:128]=k_ref[...]
        first,count=near_span(full)
        table=tab_ref[0,0]
        wide_ref[:,:first*128]=jnp.broadcast_to(table[0:1,31:32],(128,first*128))
        for c in range(count):
            wide_ref[:,(first+c)*128:(first+c+1)*128]=lookup(table,nidx_ref[:,c*128:(c+1)*128])
        rest=2*full-(first+count)*128
        wide_ref[:,2*full-rest:]=jnp.broadcast_to(table[0:1,15:16],(128,rest))
    @pl.when(before%nb==0)
    def _():
        vt_ref[0:128,:]=v_ref[...].T
    scale=LOG2E/UNIT
    def body(cur_ref,prev_ref):
        rowi=lax.broadcasted_iota(jnp.int32,(128,IB),0)
        qt=(q_ref[...]*jnp.asarray(0.125*UNIT,BF)).T
        qh=[jnp.concatenate([jnp.where((rowi<64)==(h==0),qt,jnp.zeros_like(qt)),jnp.ones_like(qt)],axis=0) for h in range(2)]
        mx=[top_ref[h:h+1,:]*scale for h in range(2)]
        top=[jnp.full((8,IB),-jnp.inf,F32)]*2
        lhs=[jnp.concatenate([vt_ref[64*h:64*h+64,:],vt_ref[128:144,:]],axis=0) for h in range(2)]
        acc=[jnp.zeros((80,IB),F32)]*2
        for m in range(full//FC):
            rows=slice(m*FC,(m+1)*FC)
            raw=[nn(ka_ref[rows,:],qh[h]) for h in range(2)]
            for h in range(2):
                p=jnp.exp2(prev_ref[h,rows,:]*scale-mx[h]).astype(BF)
                p_ref[h,0,rows,:]=p
                acc[h]=acc[h]+nn(lhs[h][:,rows],p)
            near=jnp.concatenate([wide_ref[:,pl.ds(pl.multiple_of(b*IB+(full-w*JC),128),IB)] for w in range(m*FC//JC,(m+1)*FC//JC)],axis=0)
            x=near+jnp.concatenate([lookup(tab_ref[0,1],idx_ref[0,b,rows,c*128:(c+1)*128])+lookup(tab_ref[0,1],idx_ref[1,b,rows,c*128:(c+1)*128]) for c in range(IB//128)],axis=1)
            for h in range(2):
                y=(x&0xffff) if h==0 else lax.shift_right_logical(x,16)
                s=raw[h]+y.astype(F32)
                cur_ref[h,rows,:]=s
                top[h]=jnp.maximum(top[h],jnp.max(s.reshape(FC//8,8,IB),axis=0))
        outs=[]
        for h in range(2):
            top_ref[h:h+1,:]=jnp.max(top[h],axis=0,keepdims=True)
            inv=1.0/acc[h][64:65]
            linv_ref[0,h:h+1,:]=inv
            outs.append(acc[h][:64]*inv)
        ctx_ref[...]=jnp.concatenate(outs,axis=0).T.astype(BF)
    @pl.when(t%2==0)
    def _(): body(s0_ref,s1_ref)
    @pl.when(t%2==1)
    def _(): body(s1_ref,s0_ref)

def fwd_attention(q,k,v,qcol,kcol,vcol,length,crow,ccol,tab,nidx,heads=12):
    full=q.shape[0]; width=heads*64; pairs=heads//2; nb=full//IB; last=pairs*nb-1
    now=lambda t: jnp.minimum(t,last)
    was=lambda t: jnp.maximum(t-1,0)
    return pl.pallas_call(
        fwd_kernel, grid=(pairs*nb+1,),
        in_specs=[pl.BlockSpec(memory_space=pltpu.SMEM),
          pl.BlockSpec((IB,128),lambda t:(now(t)%nb,qcol+now(t)//nb)),
          pl.BlockSpec((full,128),lambda t:(0,kcol+now(t)//nb)),
          pl.BlockSpec((full,128),lambda t:(0,vcol+was(t)//nb)),
          pl.BlockSpec((2,IB),lambda t:(0,now(t)%nb)),
          pl.BlockSpec((2,full,128),lambda t:(0,0,0)),
          pl.BlockSpec((1,2,8,128),lambda t:(now(t)//nb,0,0,0)),
          pl.BlockSpec((128,nidx.shape[1]),lambda t:(0,0))],
        out_specs=[pl.BlockSpec((IB,128),lambda t:(was(t)%nb,was(t)//nb)),
          pl.BlockSpec((2,1,full,IB),lambda t:(was(t)//nb,was(t)%nb,0,0)),
          pl.BlockSpec((1,8,IB),lambda t:(was(t)//nb,0,was(t)%nb))],
        out_shape=[jax.ShapeDtypeStruct((full,width),BF),
          jax.ShapeDtypeStruct((heads,nb,full,IB),BF),
          jax.ShapeDtypeStruct((pairs,8,full),F32)],
        scratch_shapes=[pltpu.VMEM((2,nb,full,IB),jnp.int32),pltpu.VMEM((128,2*full),jnp.int32),
          pltpu.VMEM((144,full),BF),pltpu.VMEM((full,256),BF),pltpu.VMEM((2,full,IB),F32),pltpu.VMEM((2,full,IB),F32),
          pltpu.VMEM((8,IB),F32)],
        compiler_params=pltpu.CompilerParams(vmem_limit_bytes=48*1024*1024),
        cost_estimate=pl.CostEstimate(flops=1000,bytes_accessed=1000,transcendentals=0),
        name="attend",
    )(length,q,k,v,crow,ccol,tab,nidx)

def bwd_kernel(q_ref,k_ref,v_ref,go_ref,ctx_ref,p_ref,linv_ref,
               g3_ref,ds_ref,diag_ref,
               kt_ref,acc_ref,wide_ref,gp_ref):
    g=pl.program_id(0); b=pl.program_id(1); nb=pl.num_programs(1)
    full=k_ref.shape[0]
    nj=full//JC
    @pl.when(b==0)
    def _():
        kt_ref[...]=k_ref[...].T
        acc_ref[...]=jnp.zeros_like(acc_ref)
        wide_ref[...]=jnp.zeros_like(wide_ref)
    gt=go_ref[...].astype(F32).T
    ct=ctx_ref[...].astype(F32).T
    rowi=lax.broadcasted_iota(jnp.int32,(128,IB),0)
    inv=jnp.where(rowi<64,jnp.broadcast_to(linv_ref[0,0:1,:],(128,IB)),jnp.broadcast_to(linv_ref[0,1:2,:],(128,IB)))
    gs=gt*inv
    pr=gs*ct
    gsb=gs.astype(BF)
    gos=gs.T.astype(BF)
    lane=lax.broadcasted_iota(jnp.int32,(IB,128),1)
    q2=q_ref[...]
    zero=jnp.zeros_like(q2)
    qs=[];gg=[];dqs=[];dds=[]
    for h in range(2):
        keep=(lane<64)==(h==0)
        qs.append(jnp.where(keep,q2,zero)); gg.append(jnp.where(keep,gos,zero))
        dd=jnp.sum(pr[64*h:64*h+64],axis=0,keepdims=True)
        gh=jnp.where((rowi<64)==(h==0),gsb,jnp.zeros_like(gsb))
        gp_ref[h]=nn(v_ref[...],gh)
        dds.append(dd)
    for h in range(2):
        for m in range(nj):
            rows=slice(m*JC,(m+1)*JC)
            ds=p_ref[h,0,rows,:].astype(F32)*(gp_ref[h,rows,:]-dds[h])
            ds_ref[h,0,rows,:]=ds.astype(BF)
            sl=pl.ds(pl.multiple_of(b*IB+(full-m*JC),128),IB)
            wide_ref[h,:,sl]=wide_ref[h,:,sl]+ds
        dqs.append(nn(kt_ref[64*h:64*h+64,:],ds_ref[h,0]))
    qcat=jnp.concatenate(qs,axis=0); gcat=jnp.concatenate(gg,axis=0)
    acc_ref[0]+=nn(jnp.concatenate([ds_ref[0,0],ds_ref[1,0]],axis=1),qcat)
    acc_ref[1]+=nn(jnp.concatenate([p_ref[0,0],p_ref[1,0]],axis=1),gcat)
    g3_ref[0,pl.ds(pl.multiple_of(b*IB,IB),IB),:]=(jnp.concatenate(dqs,axis=0)*0.125).T.astype(BF)
    @pl.when(b==nb-1)
    def _():
        g3_ref[1]=(acc_ref[0]*0.125).astype(BF)
        g3_ref[2]=acc_ref[1].astype(BF)
        for h in range(2):
            tot=jnp.zeros((8,2*full),F32)
            for r in range(16):
                x=wide_ref[h,r*8:(r+1)*8,:]
                tot=tot+pltpu.roll(x,2*full-r*8,1) if r else tot+x
            one=tot[0:1]
            for r in range(1,8):
                one=one+pltpu.roll(tot[r:r+1],2*full-r,1)
            diag_ref[0,h:h+1,:]=one

def bwd_attention(q,k,v,qcol,kcol,vcol,go,ctx,p,linv,heads=12):
    full=q.shape[0]; width=heads*64; pairs=heads//2; nb=full//IB
    return pl.pallas_call(
        bwd_kernel, grid=(pairs,nb),
        in_specs=[pl.BlockSpec((IB,128),lambda g,b:(b,qcol+g)),
          pl.BlockSpec((full,128),lambda g,b:(0,kcol+g)),
          pl.BlockSpec((full,128),lambda g,b:(0,vcol+g)),
          pl.BlockSpec((IB,128),lambda g,b:(b,g)),
          pl.BlockSpec((IB,128),lambda g,b:(b,g)),
          pl.BlockSpec((2,1,full,IB),lambda g,b:(g,b,0,0)),
          pl.BlockSpec((1,8,IB),lambda g,b:(g,0,b))],
        out_specs=[pl.BlockSpec((3,full,128),lambda g,b:(0,0,g)),
          pl.BlockSpec((2,1,full,IB),lambda g,b:(g,b,0,0)),
          pl.BlockSpec((1,8,2*full),lambda g,b:(g,0,0))],
        out_shape=[jax.ShapeDtypeStruct((3,full,width),BF),
          jax.ShapeDtypeStruct((heads,nb,full,IB),BF),
          jax.ShapeDtypeStruct((pairs,8,2*full),F32)],
        scratch_shapes=[pltpu.VMEM((128,full),BF),pltpu.VMEM((2,full,128),F32),pltpu.VMEM((2,128,2*full),F32),pltpu.VMEM((2,full,IB),F32)],
        compiler_params=pltpu.CompilerParams(vmem_limit_bytes=48*1024*1024),
        cost_estimate=pl.CostEstimate(flops=1000,bytes_accessed=1000,transcendentals=0),
        input_output_aliases={5:1}, name="attend_back",
    )(q,k,v,go,ctx,p,linv)

THRESH=[-8192]+[1-e for e in reversed(FAR_EDGES)]+list(FAR_EDGES)
def hist_kernel(ds_ref, crow_ref, ccol_ref, out_ref, acc_ref, lhs_ref, *, heads, dt):
    t=pl.program_id(0)
    nb=ds_ref.shape[1]
    sub=ds_ref.shape[2]//16
    @pl.when(t==0)
    def _(): acc_ref[...]=jnp.zeros_like(acc_ref)
    one=jnp.ones((16,IB),BF); zero=jnp.zeros((16,IB),BF)
    for u in range(sub):
        total=None
        for kb in range(nb):
            parts=[]
            for kind in range(2):
                row=jnp.broadcast_to(crow_ref[kind:kind+1,kb*IB:(kb+1)*IB],(16,IB)).astype(dt)
                col=jnp.concatenate([ccol_ref[kind,u*16:(u+1)*16,:]]*(IB//128),axis=1)
                less=row-col.astype(dt)
                for e in range(32):
                    parts.append(jnp.where(less<=jnp.asarray(-THRESH[min(e,30)],dt),one,zero))
            lhs_ref[u%2,:,kb*IB:(kb+1)*IB]=jnp.concatenate(parts,axis=0)
        rhs=jnp.concatenate([ds_ref[:,kb,u*16:(u+1)*16,:].reshape(heads*16,IB) for kb in range(nb)],axis=1)
        acc_ref[...]+=nt(lhs_ref[u%2],rhs)
    @pl.when(t==pl.num_programs(0)-1)
    def _():
        r=lax.broadcasted_iota(jnp.int32,(1024,heads*16),0); c=lax.broadcasted_iota(jnp.int32,(1024,heads*16),1)
        a=jnp.where((r%16)==(c%16),acc_ref[...],0.0)
        a=jnp.sum(a.reshape(64,16,heads*16),axis=1)
        out_ref[...]=a
def hist(ds,crow,ccol,heads=12,jb=32,dt=jnp.int32,part=0,parts=1):
    nb,full=ds.shape[1:3]; steps=full//jb//parts; at=part*steps
    return pl.pallas_call(functools.partial(hist_kernel,heads=heads,dt=dt),grid=(steps,),
        in_specs=[pl.BlockSpec((heads,nb,jb,IB),lambda t:(0,0,t+at,0)),
          pl.BlockSpec((2,full),lambda t:(0,0)),
          pl.BlockSpec((2,jb,128),lambda t:(0,t+at,0))],
        out_specs=pl.BlockSpec((64,heads*16),lambda t:(0,0)),
        out_shape=jax.ShapeDtypeStruct((64,heads*16),F32),
        scratch_shapes=[pltpu.VMEM((1024,heads*16),F32),pltpu.VMEM((2,1024,full),BF)],
        compiler_params=pltpu.CompilerParams(vmem_limit_bytes=48*1024*1024),
        cost_estimate=pl.CostEstimate(flops=HISTF,bytes_accessed=1000,transcendentals=0),
        name="bucket_sums")(ds,crow,ccol)

def np_level(d,edges):
    a=np.abs(d); r=np.zeros(d.shape,np.int32)
    for e in edges: r+=(a>=e)
    return r+16*(d>0)
def lanes_of():
    lane=np.arange(128)
    e=(lane%32)//2; half=lane%2
    a=np.where(e==0,0,np.where(e==1,1,2**np.maximum(e-1,0)+half*2**np.maximum(e-2,0)))
    return np_level(np.where((lane//32)%2==1,a,-a),FAR_EDGES)
def tables(bias_tables):
    near=np.arange(128)%32; far=lanes_of()
    spot=np.arange(96)
    hot=np.stack([spot==near[:,None],spot==(np.where(np.arange(128)<64,32,64)+far)[:,None]])
    t=jnp.einsum('klb,bh->hkl',jnp.asarray(hot,BF),bias_tables.reshape(96,-1),preferred_element_type=F32)
    t=jnp.round((t+4.0)*UNIT).astype(jnp.int32)
    t=t[0::2]+(t[1::2]<<16)
    return jnp.broadcast_to(t[:,:,None,:],(t.shape[0],2,8,128))
def near_span(full):
    kept=[c for c in range(2*full//128) if full-128*c-127<NEAR_EDGES[-1] and full-128*c+127>-NEAR_EDGES[-1]]
    return kept[0],len(kept)
def near_idx(full):
    first,count=near_span(full)
    r=lax.broadcasted_iota(jnp.int32,(128,count*128),0); u=first*128+lax.broadcasted_iota(jnp.int32,(128,count*128),1)
    return level(r+full-u,NEAR_EDGES)


from jax.sharding import PartitionSpec as P

BOXQ = 1000
BOTH = ("docs", "half")
TIE = -1


def fourier(coords):
    scaled = coords.astype(F32) / BOXQ
    freqs = (jnp.arange(16, dtype=F32) + 1.0) * math.pi
    angle = scaled[:, :, None] * freqs[None, None, :]
    waves = jnp.concatenate([jnp.sin(angle), jnp.cos(angle)], axis=2)
    return jnp.transpose(waves, (1, 0, 2)).reshape(coords.shape[1], 128)


def layer_norm(resid, gain, shift):
    centre = resid - jnp.mean(resid, axis=-1, keepdims=True)
    spread = jnp.mean(centre * centre, axis=-1, keepdims=True)
    return centre * lax.rsqrt(spread + 1e-06) * gain + shift


def gelu_pair(x):
    bell = jnp.exp2(x * x * (-0.5 * LOG2E))
    t = 1.0 / (1.0 + (0.3275911 * math.sqrt(0.5)) * jnp.abs(x))
    poly = t * (0.254829592 + t * (-0.284496736 + t * (1.421413741 + t * (-1.453152027 + t * 1.061405429))))
    tail = 0.5 * poly * bell
    cdf = jnp.where(x < 0, tail, 1.0 - tail)
    return x * cdf, cdf + x * bell * (1.0 / math.sqrt(2.0 * math.pi))


def inner(left, right):
    return lax.dot_general(left, right, (((0,), (0,)), ((), ())), preferred_element_type=F32)


def far_table(sums):
    total = sums[0]
    count = len(FAR_EDGES)
    below = [total - sums[count - i] for i in range(count)]
    above = [sums[count + 1 + i] for i in range(count)]
    zero = jnp.zeros_like(total)
    rows = [total - below[0] - above[0]]
    for side in (below, above):
        edges = side + [zero]
        rows += [edges[i] - edges[i + 1] for i in range(count)]
        if side is below:
            rows.append(zero)
    return jnp.stack(rows)


def swap(part, me):
    own = jnp.where(me == 0, part[0], part[1])
    other = jnp.where(me == 0, part[1], part[0])
    came = lax.ppermute(other, "half", [(0, 1), (1, 0)])
    return jnp.concatenate([jnp.where(me == 0, own, came), jnp.where(me == 0, came, own)], axis=0)


def unswap(whole, me):
    rows = whole.shape[0] // 2
    own = jnp.where(me == 0, whole[:rows], whole[rows:])
    other = jnp.where(me == 0, whole[rows:], whole[:rows])
    came = lax.ppermute(other, "half", [(0, 1), (1, 0)])
    return jnp.stack([jnp.where(me == 0, own, came), jnp.where(me == 0, came, own)])


class Route:
    def __init__(self):
        docs = lax.axis_size("docs")
        bits = [("docs", 1 << i) for i in range(docs.bit_length() - 1)]
        self.core = bits[0]
        y = ("half", 1)
        self.orders = [bits[1:2] + [y] + bits[2:], [y] + bits[1:], bits[2:] + bits[1:2] + [y]]
        self.all = bits + [y]
        self.pieces = docs * 2 // 2

    def mine(self, step):
        return (lax.axis_index(step[0]) // step[1]) % 2

    def move(self, x, step):
        axis, bit = step
        return lax.ppermute(x, axis, [(i, i ^ bit) for i in range(lax.axis_size(axis))])

    def product(self, left, right):
        mine = self.mine(self.core)
        cols = left.shape[1] // 2
        dot = lambda at: jnp.einsum("td,...tf->...df", lax.dynamic_slice_in_dim(left, at * cols, cols, 1), right,
                                    preferred_element_type=F32)
        send = dot(1 - mine).astype(BF)
        keep = dot(mine)
        return (keep + self.move(send, self.core).astype(F32)).astype(BF)

    def scatter(self, x, step):
        mine = self.mine(step)
        half = x.shape[0] // 2
        send = lax.dynamic_slice_in_dim(x, (1 - mine) * half, half, 0)
        keep = lax.dynamic_slice_in_dim(x, mine * half, half, 0)
        return (keep.astype(F32) + self.move(send, step).astype(F32)).astype(BF)

    def gather(self, x, step):
        mine = self.mine(step)
        came = self.move(x, step)
        return jnp.concatenate([jnp.where(mine == 0, x, came), jnp.where(mine == 0, came, x)], axis=0)

    def total(self, parts, between=None, last=None):
        rows = [p.shape[0] // self.pieces for p in parts]
        x = jnp.concatenate([p.reshape(self.pieces, r, p.shape[1]) for p, r in zip(parts, rows)], axis=1)
        count = x.shape[1]
        x = jnp.pad(x, ((0, 0), (0, -count % 16), (0, 0)))
        cut = x.shape[1] // 2
        lanes = [x[:, :cut], x[:, cut:]]
        hold = lambda i, lanes: between(i, lanes) if between and i < 7 else lanes
        lanes = hold(0, lanes)
        stages = len(self.orders[0])
        for i in range(stages):
            lanes = hold(1 + i, lanes)
            lanes = [self.scatter(x, order[i]) for x, order in zip(lanes, self.orders)]
        for i in reversed(range(stages)):
            lanes = hold(2 * stages - i, lanes) if stages == 4 else lanes
            lanes = [self.gather(x, order[i]) for x, order in zip(lanes, self.orders)]
        lanes = last(lanes) if last else lanes
        came = [self.move(x, self.core) for x in lanes]
        mine = self.mine(self.core)
        own, came = jnp.concatenate(lanes, axis=1), jnp.concatenate(came, axis=1)
        whole = jnp.concatenate([jnp.where(mine == 0, own, came), jnp.where(mine == 0, came, own)], axis=0)
        out = []
        at = 0
        for p, r in zip(parts, rows):
            out.append(whole[:, at:at + r].reshape(-1, p.shape[1]).astype(F32))
            at += r
        return out

    def small(self, parts):
        sizes = [p.size for p in parts]
        flat = jnp.concatenate([p.reshape(-1) for p in parts])
        count = flat.shape[0]
        flat = jnp.pad(flat, (0, -count % 1024)).reshape(-1, 128)
        for step in self.all:
            flat = flat + self.move(flat, step)
        flat = flat.reshape(-1)
        out = []
        at = 0
        for p, n in zip(parts, sizes):
            out.append(flat[at:at + n].reshape(p.shape))
            at += n
        return out


def shards(hidden_in, boxes, lengths, cotangent, layout_weight, qkv_weight, qv_bias, bias_tables, out_weight,
           out_bias, norm1_gain, norm1_bias, ff_in, ff_in_bias, ff_out, ff_out_bias, norm2_gain, norm2_bias):
    width = hidden_in.shape[2]
    full = boxes.shape[2]
    heads = bias_tables.shape[2]
    me = lax.axis_index("half")
    route = Route()
    hidden = swap(hidden_in, me)
    box = lax.dynamic_index_in_dim(boxes, me, 1, keepdims=False)
    length = lax.dynamic_slice_in_dim(lengths, me, 1, 0)
    feats = fourier(box).astype(BF)
    crow = jnp.stack([box[0] + box[2], box[1] + box[3]])
    ccol = jnp.broadcast_to(crow[:, :, None], (2, full, 128))
    packed = tables(bias_tables)
    skew = near_idx(full)
    bias3 = jnp.concatenate([qv_bias[0], jnp.zeros_like(qv_bias[0]), qv_bias[1]]).astype(F32)
    hidden, feats, ccol, packed, skew, bias3 = lax.optimization_barrier((hidden, feats, ccol, packed, skew, bias3))
    start = hidden.astype(F32) + nn(feats, layout_weight)
    start_low = start.astype(BF)
    qkv = (nn(start_low, qkv_weight) + bias3).astype(BF)
    pairs = heads // 2
    context, probs, linv = fwd_attention(
        qkv, qkv, qkv, 0, pairs, 2 * pairs, length, crow, ccol, packed, skew, heads)
    upstream = swap(cotangent, me).astype(F32)
    attended = nn(context, out_weight) + out_bias.astype(F32)
    mid, norm1_pull = jax.vjp(layer_norm, start + attended, norm1_gain.astype(F32), norm1_bias.astype(F32))
    mid_low = mid.astype(BF)
    hidden_pre = nn(mid_low, ff_in) + ff_in_bias.astype(F32)
    activated, slope = gelu_pair(hidden_pre)
    activated = activated.astype(BF)
    activated, slope = lax.optimization_barrier((activated, slope.astype(BF)))
    branch = nn(activated, ff_out) + ff_out_bias.astype(F32)
    result, norm2_pull = jax.vjp(layer_norm, mid + branch, norm2_gain.astype(F32), norm2_bias.astype(F32))
    layer_out = unswap(result.astype(BF), me)
    grad_r2, gain2_grad, shift2_grad = norm2_pull(upstream)
    grad_ff = grad_r2.astype(BF)
    ffout_part = inner(activated, grad_ff).astype(BF)
    ffoutb_grad = jnp.sum(grad_ff.astype(F32), axis=0)
    grad_inner = (nt(grad_ff, ff_out) * slope.astype(F32)).astype(BF)
    ffin_part = inner(mid_low, grad_inner).astype(BF)
    ffinb_grad = nn(jnp.ones((8, full), BF), grad_inner)[0]
    grad_mid = grad_r2 + nt(grad_inner, ff_in)
    grad_r1, gain1_grad, shift1_grad = norm1_pull(grad_mid)
    grad_att = grad_r1.astype(BF)
    outw_part = inner(context, grad_att).astype(BF)
    outb_grad = jnp.sum(grad_att.astype(F32), axis=0)
    grad_context = nt(grad_att, out_weight).astype(BF)
    early = (ffout_part, ffin_part, outw_part)
    grad_context = lax.optimization_barrier((*early, grad_context))[-1]
    early = lax.psum(early, BOTH)
    grad3, gscores, diag = bwd_attention(
        qkv, qkv, qkv, 0, pairs, 2 * pairs, grad_context, context, probs, linv, heads)
    qkv_part = route.product(start_low, grad3)
    qvb_grad = jnp.sum(grad3.astype(F32), axis=1)[0::2]
    grad_start = (grad_r1 + sum(nt(grad3[c], qkv_weight[:, c * width:(c + 1) * width]) for c in range(3))).astype(BF)
    input_grad = unswap(grad_start, me)
    lay_part = route.product(feats, grad_start)
    plan = [1, 1, 1, 1, 1, 1, 2]
    bucket_parts = []

    def between(i, lanes):
        row = crow
        if i:
            row, *lanes = lax.optimization_barrier((crow, *lanes))
        for _ in range(plan[i]):
            bucket_parts.append(hist(gscores, row, ccol, heads, dt=jnp.int16, part=len(bucket_parts), parts=sum(plan)))
        return lanes

    late = [qkv_part[0], qkv_part[1], qkv_part[2], lay_part]
    def last(lanes):
        nonlocal early
        *early, a, b = lax.optimization_barrier((*early, *lanes))
        return [a, b]

    groups = route.total(late, between, last)
    assert len(bucket_parts) == sum(plan)
    sums = jnp.sum(sum(bucket_parts).reshape(2, 32, heads, 16), axis=3)
    offset = lax.broadcasted_iota(jnp.int32, (2 * full, 32), 0)
    bucket = lax.broadcasted_iota(jnp.int32, (2 * full, 32), 1)
    near_hot = (level(full - offset, NEAR_EDGES) == bucket).astype(F32)
    diag = diag[:, :2].reshape(heads, 2 * full)
    near_grad = lax.dot_general(near_hot, diag, (((0,), (1,)), ((), ())), precision=lax.Precision.HIGHEST)
    table_grad = jnp.stack([near_grad, far_table(sums[0]), far_table(sums[1])])

    qkv_total = jnp.concatenate(groups[:3], axis=1)
    lay_total = groups[3]
    (ffinb_total, ffoutb_total, gain2_total, shift2_total, outb_total, gain1_total, shift1_total, qvb_total,
     table_total) = route.small([ffinb_grad, ffoutb_grad, gain2_grad, shift2_grad, outb_grad, gain1_grad, shift1_grad,
                                 qvb_grad, table_grad])
    ffout_total, ffin_total, outw_total = (x.astype(F32) for x in early)
    return (layer_out, input_grad, lay_total, qkv_total, qvb_total, table_total, outw_total,
            outb_total, gain1_total, shift1_total, ffin_total, ffinb_total, ffout_total, ffoutb_total,
            gain2_total, shift2_total)


def solution(mesh):
    placed = (P("docs", "half", None), P(None, "docs", None), P("docs"), P("docs", "half", None)) + (P(),) * 14
    return jax.shard_map(
        shards, mesh=mesh, in_specs=placed,
        out_specs=(P("docs", "half", None), P("docs", "half", None)) + (P(),) * 14, check_vma=False)
```
